32 devices in a mesh: group: 2 (over x), particle: 2 (over core), strip: 8 (over z, y).
Axes of the slice: x: 2, y: 2, z: 4, core: 2. Of those that a mesh axis runs over, the one named last changes fastest.
Arguments:
- ensemble: float32 [16, 3, 64, 4096], P(('group', 'particle'), None, 'strip'), parts along dimension 0, may hold values from -1 to 1
- offspring: int32 [16], P('group'), parts along dimension 0, may hold values from 0 to 2, as said below
- observations: float32 [128, 128], P(('group', 'strip')), parts along dimension 0, may hold values from -6 to 6
- obs_cols: int32 [128, 128], P(('group', 'strip')), parts along dimension 0, may hold values from 0 to 4095
- obs_precision: float32 [128, 128], P(('group', 'strip')), parts along dimension 0, may hold values from 0.3 to 3
Outputs:
- forecast: float32 [16, 3, 64, 4096], P(('group', 'particle'), None, 'strip'), parts along dimension 0
- log_weights: float32 [16], P(('group', 'particle')), parts along dimension 0
The draws below stay inside these ranges and needn't reach their ends.
There are 2 independent parts, one for each index of `group`. The reference program is written for one: setup_inputs(seed, part) draws one part's arguments, and reference() takes and returns one part's arrays. A program takes and returns all parts, laid end to end along the dimension named above; each array names one. Nothing has to cross between parts.
Inputs may be any that keep to these rules, and one draw needn't show every extreme that they name: `offspring`: nonnegative copy counts that sum to 8.
All inputs are finite; a program needn't handle non-finite values.
Results may differ from the reference program's by a relative error of at most 0.00002.
Values sent between devices are 32-bit elements; how exact they have to be, the bound alone decides.
No kernel may reach another device: no remote copies, remote signals or barrier semaphores. Data moves between devices by JAX's collectives and lax.ppermute only.
A program may use at most 64 MiB of HBM per device.

```python
import math
import jax
import jax.numpy as jnp

COLS = 4096
OBS = 128
STEPS = 3
PARTICLES = 8
NY = 64


def draw_offspring(key, part):
    key = jax.random.fold_in(key, 7)
    order_key = jax.random.fold_in(key, 1)
    count_key = jax.random.fold_in(key, 2)
    order = jax.random.permutation(order_key, PARTICLES).astype(jnp.int32)
    halves = jax.random.randint(count_key, (PARTICLES // 2,), 0, 3).astype(jnp.int32)
    halves = halves.at[0].set(2)
    counts = jnp.concatenate([halves, 2 - halves]).astype(jnp.int32)
    return jnp.zeros((PARTICLES,), jnp.int32).at[order].set(counts)


def place_ends(entries, own_key, least, largest):
    shape = entries.shape
    index_at = [jax.random.randint(jax.random.fold_in(own_key, axis), (), 0, shape[axis]) for axis in range(len(shape))]
    entries = entries.at[tuple(index_at)].set(least)
    longest = shape.index(max(shape))
    index_at[longest] = (index_at[longest] + 1) % shape[longest]
    return entries.at[tuple(index_at)].set(largest)


def block_levels(stream_key, shape, cuts, smallest, high):
    loudness = 1.0
    for position, blocks in cuts:
        draws = jax.random.uniform(jax.random.fold_in(jax.random.fold_in(stream_key, 6), position), (blocks,), jnp.float32, smallest / len(cuts), high / len(cuts))
        loudness = loudness * jnp.repeat(jnp.exp(draws), shape[position] // blocks).reshape((-1,) + (1,) * (len(shape) - 1 - position))
    return loudness


def bell_draw(own_key, dims, spread, bound, cuts=(), kind=jnp.bfloat16):
    drawn = jax.random.normal(own_key, dims, jnp.float32) * spread
    if len(cuts) > 0:
        drawn = block_levels(own_key, dims, cuts, -0.22, 0.18) * drawn
    return jnp.clip(drawn, min=-bound, max=bound).astype(kind)


def setup_inputs(seed: int = 0, part: int = 0) -> dict:
    splits = jax.random.split(jax.random.key(seed), 6)
    part_splits = jax.random.split(jax.random.fold_in(splits[5], part), 6)
    return {
        "ensemble": bell_draw(part_splits[0], (PARTICLES, 3, NY, COLS), 0.2, 1.0, ((0, 2), (2, 8)), jnp.float32),
        "offspring": draw_offspring(jax.random.fold_in(jax.random.fold_in(splits[5], part), 71), part),
        "observations": bell_draw(part_splits[2], (NY, OBS), 1.0, 6.0, ((0, 8),), jnp.float32),
        "obs_cols": place_ends(jax.random.randint(part_splits[3], (NY, OBS), 0, COLS), jax.random.fold_in(part_splits[3], 1), 0, COLS - 1).astype(jnp.int32),
        "obs_precision": jnp.clip(jnp.exp(math.log(3.0) - 2.3025851 * jax.random.uniform(part_splits[4], (NY, OBS), jnp.float32) ** block_levels(part_splits[4], (NY, OBS), ((0, 8),), -0.2, 0.2)), 0.3, 3.0),
    }


DT = 0.4


def wrap_rows(fields):
    return jnp.concatenate([fields[..., -1:, :], fields, fields[..., :1, :]], axis=-2)


def tendency(padded, coriolis):
    eta = padded[..., 0, :, :]
    east = padded[..., 1, :, :]
    north = padded[..., 2, :, :]
    depth = 1.0 + eta

    def along_x(field):
        inner = field[..., 1:-1, :]
        return 0.5 * (jnp.roll(inner, -1, axis=-1) - jnp.roll(inner, 1, axis=-1))

    def along_y(field):
        return 0.5 * (field[..., 2:, :] - field[..., :-2, :])

    east_c = east[..., 1:-1, :]
    north_c = north[..., 1:-1, :]
    eta_t = -(along_x(depth * east) + along_y(depth * north))
    east_t = -(east_c * along_x(east) + north_c * along_y(east)) + coriolis * north_c - along_x(eta)
    north_t = -(east_c * along_x(north) + north_c * along_y(north)) - coriolis * east_c - along_y(eta)
    return jnp.stack([eta_t, east_t, north_t], axis=-3)


def reference(ensemble, offspring, observations, obs_cols, obs_precision):
    cumulative = jnp.cumsum(offspring).astype(jnp.int32)
    slots = jnp.arange(PARTICLES, dtype=jnp.int32)
    source = jnp.sum((cumulative[None, :] <= slots[:, None]).astype(jnp.int32), axis=1).astype(jnp.int32)
    state = jnp.take(ensemble, source, axis=0)
    rows = jnp.arange(NY, dtype=jnp.int32).astype(jnp.float32)
    coriolis = (0.3 + 0.4 * ((rows + 0.5) / NY - 0.5))[:, None]
    for step in range(STEPS):
        first = state + DT * tendency(wrap_rows(state), coriolis)
        second = 0.75 * state + 0.25 * (first + DT * tendency(wrap_rows(first), coriolis))
        state = state / 3.0 + (2.0 / 3.0) * (second + DT * tendency(wrap_rows(second), coriolis))
    eta = state[:, 0]
    index = jnp.broadcast_to(obs_cols[None], (PARTICLES, NY, OBS))
    picked = jnp.take_along_axis(eta, index, axis=-1)
    weight = obs_precision * (1.0 + 2.0 * (rows + 0.5) / NY)[:, None]
    misfit = observations[None] - picked
    total = jnp.sum(weight[None] * misfit * misfit, axis=(1, 2))
    log_weights = -0.5 * total / (NY * OBS)
    return state, log_weights
```

```python
import functools

import jax
import jax.numpy as jnp
from jax import lax
from jax.experimental import pallas as pl
from jax.experimental.pallas import tpu as pltpu
from jax.sharding import PartitionSpec as P

STEPS = 3
DT = 0.4
HALF = 0.5 * DT
DEPTH = 3 * STEPS
LANES = 128
TILE = 8
UNROLL = 4

VMEM = pl.BlockSpec(memory_space=pltpu.VMEM)
SMEM = pl.BlockSpec(memory_space=pltpu.SMEM)
ANY = pl.BlockSpec(memory_space=pl.ANY)


def pick_kernel(index_ref, own_ref, other_ref, *rest, count):
    outs, sems = rest[:count], rest[count]
    own = own_ref.shape[0]
    for k in range(count):
        at = index_ref[k]

        @pl.when(at < own)
        def _():
            pltpu.make_async_copy(own_ref.at[jnp.minimum(at, own - 1)], outs[k], sems.at[k]).start()

        @pl.when(at >= own)
        def _():
            pltpu.make_async_copy(
                other_ref.at[jnp.maximum(at - own, 0)], outs[k], sems.at[k]
            ).start()

    for k in range(count):
        pltpu.make_async_copy(own_ref.at[0], outs[k], sems.at[k]).wait()


def pick(index, own, other):
    count = index.shape[0]
    block = jax.ShapeDtypeStruct(own.shape[1:], own.dtype)
    return pl.pallas_call(
        functools.partial(pick_kernel, count=count),
        out_shape=[block] * count,
        in_specs=[SMEM, ANY, ANY],
        out_specs=[ANY] * count,
        scratch_shapes=[pltpu.SemaphoreType.DMA((count,))],
    )(index, own, other)


def pack_kernel(par_ref, own_ref, got_ref, up_ref, down_ref):
    cols = own_ref.shape[2]
    part = cols // TILE

    def fill(top, bottom):
        up_ref[:, :, :cols] = bottom[...]
        down_ref[:, :, :cols] = top[...]
        for f in range(3):
            for q in range(TILE):
                up_ref[f, q : q + 1, cols:] = top[f, TILE - 1 : TILE, q * part : (q + 1) * part]
                down_ref[f, q : q + 1, cols:] = bottom[f, 0:1, q * part : (q + 1) * part]

    @pl.when(par_ref[0] == 0)
    def _():
        fill(own_ref, got_ref)

    @pl.when(par_ref[0] == 1)
    def _():
        fill(got_ref, own_ref)


def pack(par, own, got):
    cols = own.shape[2]
    message = jax.ShapeDtypeStruct((3, TILE, cols + cols // TILE), own.dtype)
    return pl.pallas_call(
        pack_kernel,
        out_shape=[message, message],
        in_specs=[SMEM, VMEM, VMEM],
        out_specs=[VMEM, VMEM],
    )(par, own, got)


BASE = 16
ROWS = 48


def evaluate(src, state, dst, cor_ref, start, tiles, kind):
    ncol = src.shape[1]
    lane = lax.broadcasted_iota(jnp.int32, (TILE, LANES), 1)
    first = lane == 0
    last = lane == LANES - 1

    def one(ct, r0, cor):
        left = (ct + (ncol - 1)) % ncol
        right = (ct + 1) % ncol
        rows = pl.ds(r0, TILE)
        mid, dx, dy = [], [], []
        ee = []
        for f in range(3):
            c = src[f, ct, rows, :]
            e = pltpu.roll(jnp.where(first, src[f, right, rows, :], c), LANES - 1, 1)
            w = pltpu.roll(jnp.where(last, src[f, left, rows, :], c), 1, 1)
            n = src[f, ct, pl.ds(r0 + 1, TILE), :]
            s = src[f, ct, pl.ds(r0 - 1, TILE), :]
            mid.append(c)
            ee.append((e, w, n, s))
        eta, u, v = mid
        (eE, eW, eN, eS), (uE, uW, uN, uS), (vE, vW, vN, vS) = ee
        duy = uN - uS
        dvx = vE - vW
        dux = uE - uW
        dvy = vN - vS
        flow = (dux + dvy) + ((eE * uE - eW * uW) + (eN * vN - eS * vS))
        lu = v * (cor - duy) - u * dux - (eE - eW)
        lv = u * (cor + dvx) + v * dvy + (eN - eS)
        change = (-flow, lu, -lv)
        for f in range(3):
            if kind == 0:
                new = mid[f] + HALF * change[f]
            elif kind == 1:
                new = 0.75 * state[f, ct, rows, :] + (0.25 * mid[f] + (0.25 * HALF) * change[f])
            else:
                new = (1.0 / 3.0) * state[f, ct, rows, :] + (
                    (2.0 / 3.0) * mid[f] + (2.0 / 3.0 * HALF) * change[f]
                )
            dst[f, ct, rows, :] = new

    for t in range(tiles):
        r0 = start + t * TILE
        cor = cor_ref[pl.ds(r0, TILE), :]

        def body(i, carry):
            for k in range(UNROLL):
                one(i * UNROLL + k, r0, cor)
            return carry

        lax.fori_loop(0, ncol // UNROLL, body, 0)


def forecast_kernel(
    scalars, own, got, low, high, obs_own, obs_got, keep, send, misfit, state, s1, s2, cor_ref
):
    cols = own.shape[2]
    ncol = cols // LANES
    per = ncol // TILE
    par = scalars[0]

    def load(top, bottom):
        for f in range(3):
            for ct in range(ncol):
                at = slice(ct * LANES, (ct + 1) * LANES)
                state[f, ct, BASE : BASE + TILE, :] = top[f, :, at]
                state[f, ct, BASE + TILE : BASE + 2 * TILE, :] = bottom[f, :, at]

    @pl.when(par == 0)
    def _():
        load(own, got)

    @pl.when(par == 1)
    def _():
        load(got, own)

    for f in range(3):
        for ct in range(ncol):
            at = slice(ct * LANES, (ct + 1) * LANES)
            state[f, ct, BASE - TILE : BASE, :] = low[f, :, at]
            state[f, ct, BASE + 2 * TILE : BASE + 3 * TILE, :] = high[f, :, at]
            q = ct // per
            at = slice(cols + (ct % per) * LANES, cols + (ct % per + 1) * LANES)
            state[f, ct, BASE - TILE - 1 : BASE - TILE, :] = low[f, q : q + 1, at]
            state[f, ct, BASE + 3 * TILE : BASE + 3 * TILE + 1, :] = high[f, q : q + 1, at]

    total_rows = scalars[2]
    row = lax.broadcasted_iota(jnp.int32, (ROWS, LANES), 0) + (scalars[1] - BASE)
    row = jnp.where(row < 0, row + total_rows, row)
    row = jnp.where(row >= total_rows, row - total_rows, row).astype(jnp.float32)
    rows_f = total_rows.astype(jnp.float32)
    cor_ref[...] = 2.0 * (0.3 + 0.4 * ((row + 0.5) / rows_f - 0.5))

    for k in range(DEPTH):
        reach = DEPTH - 1 - k
        start = BASE - reach
        tiles = (2 * TILE + 2 * reach + TILE - 1) // TILE
        kind = k % 3
        src, dst = ((state, s1), (s1, s2), (s2, state))[kind]
        evaluate(src, state, dst, cor_ref, start, tiles, kind)

    def store(top, bottom):
        for f in range(3):
            for ct in range(ncol):
                at = slice(ct * LANES, (ct + 1) * LANES)
                top[f, :, at] = state[f, ct, BASE : BASE + TILE, :]
                bottom[f, :, at] = state[f, ct, BASE + TILE : BASE + 2 * TILE, :]

    @pl.when(par == 0)
    def _():
        store(keep, send)

    @pl.when(par == 1)
    def _():
        store(send, keep)

    total = jnp.zeros((TILE, LANES), jnp.float32)
    for half in range(2):
        mine = par == half
        obs = [jnp.where(mine, obs_own[k], obs_got[k]) for k in range(3)]
        where = obs[1].astype(jnp.int32)
        tile, lane = where // LANES, where % LANES
        picked = jnp.zeros((TILE, LANES), jnp.float32)
        for ct in range(ncol):
            eta = state[0, ct, BASE + half * TILE : BASE + (half + 1) * TILE, :]
            there = jnp.take_along_axis(eta, lane, axis=1)
            picked = jnp.where(tile == ct, there, picked)
        gap = obs[0] - picked
        total = total + obs[2] * gap * gap
    misfit[...] = total


def forecast(scalars, own, got, low, high, obs_own, obs_got):
    cols = own.shape[2]
    block = jax.ShapeDtypeStruct(own.shape, own.dtype)
    field = pltpu.VMEM((3, cols // LANES, ROWS, LANES), jnp.float32)
    return pl.pallas_call(
        forecast_kernel,
        out_shape=[block, block, jax.ShapeDtypeStruct((TILE, LANES), jnp.float32)],
        in_specs=[SMEM] + [VMEM] * 6,
        out_specs=[VMEM] * 3,
        scratch_shapes=[field, field, field, pltpu.VMEM((ROWS, LANES), jnp.float32)],
        compiler_params=pltpu.CompilerParams(vmem_limit_bytes=32 * 2**20),
    )(scalars, own, got, low, high, obs_own, obs_got)


def local(ensemble, offspring, observations, obs_cols, obs_precision):
    members, _, strip_rows, cols = ensemble.shape
    strips = lax.axis_size("strip")
    total_rows = strips * strip_rows
    strip = lax.axis_index("strip")
    par = strip % 2
    half = members // 2
    swap = [(i, i ^ 1) for i in range(strips)]
    up = [(i, (i + 2) % strips) for i in range(strips)]
    down = [(b, a) for a, b in up]

    total_members = offspring.shape[0]
    cumulative = jnp.cumsum(offspring)
    slots = jnp.arange(total_members, dtype=jnp.int32)
    source = jnp.sum((cumulative[None, :] <= slots[:, None]).astype(jnp.int32), axis=1)
    here = lax.axis_index("particle")

    def crossing(side):
        wanted = lax.dynamic_slice_in_dim(source, (1 - side) * members, members)
        mine = wanted // members == side
        low = jnp.min(jnp.where(mine, wanted, total_members))
        high = jnp.max(jnp.where(mine, wanted, -1))
        base = side * members
        return jnp.clip(low - base, 0, members - 1), jnp.clip(high - base, 0, members - 1)

    low_out, high_out = crossing(here)
    leaving = jnp.concatenate(
        [
            lax.dynamic_slice_in_dim(ensemble, low_out, 1, axis=0),
            lax.dynamic_slice_in_dim(ensemble, high_out, 1, axis=0),
        ]
    )
    arrived = lax.ppermute(leaving, "particle", [(0, 1), (1, 0)])
    low_in, _ = crossing(1 - here)
    wanted = lax.dynamic_slice_in_dim(source, here * members, members)
    local_at = wanted - here * members
    other_at = wanted - (1 - here) * members
    own = wanted // members == here
    index = jnp.where(own, local_at, jnp.where(other_at == low_in, members, members + 1))

    rows = (strip * strip_rows + jnp.arange(strip_rows, dtype=jnp.int32)).astype(jnp.float32)
    weight = obs_precision * (1.0 + 2.0 * (rows + 0.5) / total_rows)[:, None]
    obs_own = jnp.stack([observations, obs_cols.astype(jnp.float32), weight])
    obs_got = lax.ppermute(obs_own, "strip", swap)

    order = jnp.stack([(1 - par) * half + k for k in range(half)] + [par * half + k for k in range(half)])
    blocks = pick(jnp.take(index, order), ensemble, arrived)
    given, kept = blocks[:half], blocks[half:]
    scalars = jnp.stack([par, (strip - par) * strip_rows, jnp.int32(total_rows)]).astype(jnp.int32)

    keeps, backs, sums = [], [], []
    got = [lax.ppermute(g, "strip", swap) for g in given]
    for k in range(half):
        rising, falling = pack(scalars, kept[k], got[k])
        low = lax.ppermute(rising, "strip", up)
        high = lax.ppermute(falling, "strip", down)
        keep, send, misfit = forecast(scalars, kept[k], got[k], low, high, obs_own, obs_got)
        keeps.append(keep)
        backs.append(lax.ppermute(send, "strip", swap))
        sums.append(jnp.sum(misfit))
    total = jnp.stack(sums)
    step = 2
    while step < strips:
        total = total + lax.ppermute(total, "strip", [(i, i ^ step) for i in range(strips)])
        step *= 2
    total_got = lax.ppermute(total, "strip", swap)
    lower = par == 0
    mine, theirs = jnp.stack(keeps), jnp.stack(backs)
    state = jnp.concatenate([jnp.where(lower, mine, theirs), jnp.where(lower, theirs, mine)])
    total = jnp.concatenate([jnp.where(lower, total, total_got), jnp.where(lower, total_got, total)])
    log_weights = -0.5 * total / (total_rows * obs_cols.shape[1])
    return (state, log_weights)


def solution(mesh):
    in_specs = (
        P(("group", "particle"), None, "strip", None),
        P("group"),
        P(("group", "strip"), None),
        P(("group", "strip"), None),
        P(("group", "strip"), None),
    )
    out_specs = (P(("group", "particle"), None, "strip", None), P(("group", "particle")))
    return jax.shard_map(local, mesh=mesh, in_specs=in_specs, out_specs=out_specs, check_vma=False)
```

```python
import functools

import jax
import jax.numpy as jnp
from jax import lax
from jax.experimental import pallas as pl
from jax.experimental.pallas import tpu as pltpu
from jax.sharding import PartitionSpec as P

STEPS = 3
DT = 0.4
HALF = 0.5 * DT
DEPTH = 3 * STEPS
LANES = 128
TILE = 8
BASE = 16
ROWS = 48

VMEM = pl.BlockSpec(memory_space=pltpu.VMEM)
SMEM = pl.BlockSpec(memory_space=pltpu.SMEM)


def cost(us):
    return pl.CostEstimate(flops=0, bytes_accessed=int(us * 3.0e6), transcendentals=0)


def halves(ncol):
    cut = ncol // 2 + 2
    return (
        (list(range(cut)), list(range(cut)), list(range(1, cut - 1))),
        (
            list(range(cut, ncol)),
            list(range(cut - 2, ncol)) + [0, 1],
            list(range(cut - 1, ncol)) + [0],
        ),
    )


def at(i):
    return slice(i * LANES, (i + 1) * LANES)


def leave_kernel(offspring, ensemble, leaving, index):
    members = ensemble.shape[0]
    total = offspring.shape[0]
    here = lax.axis_index("particle")
    cumulative = []
    for i in range(total):
        cumulative.append(offspring[i] + (cumulative[-1] if i else 0))

    def source(j):
        return sum((c <= j).astype(jnp.int32) for c in cumulative)

    def span(side):
        base = side * members
        low, high = jnp.int32(members), jnp.int32(-1)
        for k in range(members):
            s = source((1 - side) * members + k) - base
            mine = (s >= 0) & (s < members)
            low = jnp.minimum(low, jnp.where(mine, s, members))
            high = jnp.maximum(high, jnp.where(mine, s, -1))
        return jnp.clip(low, 0, members - 1), jnp.clip(high, 0, members - 1)

    low, high = span(here)
    leaving[0] = ensemble[low]
    leaving[1] = ensemble[high]
    there, _ = span(1 - here)
    for k in range(members):
        s = source(here * members + k)
        own = s - here * members
        other = s - (1 - here) * members
        inside = (own >= 0) & (own < members)
        index[k] = jnp.where(inside, own, jnp.where(other == there, members, members + 1))


def leave(offspring, ensemble):
    return pl.pallas_call(
        leave_kernel,
        out_shape=[
            jax.ShapeDtypeStruct((2,) + ensemble.shape[1:], ensemble.dtype),
            jax.ShapeDtypeStruct((ensemble.shape[0],), jnp.int32),
        ],
        in_specs=[SMEM, VMEM],
        out_specs=[VMEM, SMEM],
    )(offspring, ensemble)


def pick_kernel(index, own, other, *outs, parts):
    members = own.shape[0]
    half = members // 2
    par = lax.axis_index("strip") % 2
    kept, given = outs[:half], outs[half:]

    def copy(slot, write):
        i = index[slot]

        @pl.when(i < members)
        def _():
            write(own, jnp.minimum(i, members - 1))

        @pl.when(i >= members)
        def _():
            write(other, jnp.maximum(i - members, 0))

    for k in range(half):

        def whole(ref, i):
            kept[k][...] = ref[i]

        def split(ref, i):
            for p, (first, count) in enumerate(parts):
                given[k * len(parts) + p][...] = ref[i, :, :, pl.ds(first, count)]

        copy((1 - par) * half + k, split)
        copy(par * half + k, whole)


def pick(index, own, other, parts):
    half = own.shape[0] // 2
    whole = jax.ShapeDtypeStruct(own.shape[1:], own.dtype)
    pieces = [jax.ShapeDtypeStruct(own.shape[1:3] + (c,), own.dtype) for _, c in parts]
    outs = [whole] * half + pieces * half
    got = pl.pallas_call(
        functools.partial(pick_kernel, parts=parts),
        out_shape=outs,
        in_specs=[SMEM, VMEM, VMEM],
        out_specs=[VMEM] * len(outs),
    )(index, own, other)
    return got[:half], [got[half + k * len(parts) : half + (k + 1) * len(parts)] for k in range(half)]


def pack_kernel(own_ref, got_ref, up_ref, down_ref, *, sent):
    par = lax.axis_index("strip") % 2
    count = len(sent)
    wide = count * LANES
    per = -(-count // TILE)
    first = sent[0] * LANES
    own = own_ref.at[:, :, pl.ds(first, wide)]

    def fill(top, bottom):
        up_ref[:, :, :wide] = bottom[...]
        down_ref[:, :, :wide] = top[...]
        for i in range(count):
            q, lanes = i // per, slice(wide + (i % per) * LANES, wide + (i % per + 1) * LANES)
            up_ref[:, q : q + 1, lanes] = top[:, TILE - 1 : TILE, at(i)]
            down_ref[:, q : q + 1, lanes] = bottom[:, 0:1, at(i)]

    @pl.when(par == 0)
    def _():
        fill(own, got_ref)

    @pl.when(par == 1)
    def _():
        fill(got_ref, own)


def pack(own, got, sent):
    per = -(-len(sent) // TILE)
    message = jax.ShapeDtypeStruct((3, TILE, (len(sent) + per) * LANES), own.dtype)
    return pl.pallas_call(
        functools.partial(pack_kernel, sent=sent),
        out_shape=[message, message],
        in_specs=[VMEM, VMEM],
        out_specs=[VMEM, VMEM],
        cost_estimate=cost(1.5),
    )(own, got)


def evaluate(src, state, dst, cor_ref, start, tiles, kind):
    ncol = src.shape[1]
    lane = lax.broadcasted_iota(jnp.int32, (TILE, LANES), 1)
    first = lane == 0
    last = lane == LANES - 1

    def body(t, carry):
        r0 = start + t * TILE
        rows = pl.ds(r0, TILE)
        cor = cor_ref[rows, :]
        for ct in range(ncol):
            mid, around = [], []
            for f in range(3):
                c = src[f, ct, rows, :]
                e = pltpu.roll(
                    jnp.where(first, src[f, (ct + 1) % ncol, rows, :], c), LANES - 1, 1
                )
                w = pltpu.roll(jnp.where(last, src[f, (ct - 1) % ncol, rows, :], c), 1, 1)
                n = src[f, ct, pl.ds(r0 + 1, TILE), :]
                s = src[f, ct, pl.ds(r0 - 1, TILE), :]
                mid.append(c)
                around.append((e, w, n, s))
            eta, u, v = mid
            (eE, eW, eN, eS), (uE, uW, uN, uS), (vE, vW, vN, vS) = around
            duy = uN - uS
            dvx = vE - vW
            dux = uE - uW
            dvy = vN - vS
            flow = (dux + dvy) + ((eE * uE - eW * uW) + (eN * vN - eS * vS))
            lu = v * (cor - duy) - u * dux - (eE - eW)
            lv = u * (cor + dvx) + v * dvy + (eN - eS)
            change = (-flow, lu, -lv)
            for f in range(3):
                if kind == 0:
                    new = mid[f] + HALF * change[f]
                elif kind == 1:
                    new = 0.75 * state[f, ct, rows, :] + (0.25 * mid[f] + (0.25 * HALF) * change[f])
                else:
                    new = (1.0 / 3.0) * state[f, ct, rows, :] + (
                        (2.0 / 3.0) * mid[f] + (2.0 / 3.0 * HALF) * change[f]
                    )
                dst[f, ct, rows, :] = new
        return carry

    lax.fori_loop(0, tiles, body, 0)


def forecast_kernel(*refs, worked, kept, ncol, place, total_rows, slot, slots):
    parts = max(p for p, _ in place) + 1
    own, refs = refs[0], refs[1:]
    got, low, high = refs[:parts], refs[parts : 2 * parts], refs[2 * parts : 3 * parts]
    obs_own, obs_got, keep, send, misfit, state, s1, s2, cor_ref = refs[3 * parts :]
    strip = lax.axis_index("strip")
    par = strip % 2

    def load(own_row, got_row):
        for i, ct in enumerate(worked):
            p, j = place[i]
            state[:, i, own_row : own_row + TILE, :] = own[:, :, at(ct)]
            state[:, i, got_row : got_row + TILE, :] = got[p][:, :, at(j)]

    @pl.when(par == 0)
    def _():
        load(BASE, BASE + TILE)

    @pl.when(par == 1)
    def _():
        load(BASE + TILE, BASE)

    for i in range(len(worked)):
        p, j = place[i]
        state[:, i, BASE - TILE : BASE, :] = low[p][:, :, at(j)]
        state[:, i, BASE + 2 * TILE : BASE + 3 * TILE, :] = high[p][:, :, at(j)]
        count = got[p].shape[2] // LANES
        per = -(-count // TILE)
        q, lanes = j // per, at(count + j % per)
        state[:, i, BASE - TILE - 1 : BASE - TILE, :] = low[p][:, q : q + 1, lanes]
        state[:, i, BASE + 3 * TILE : BASE + 3 * TILE + 1, :] = high[p][:, q : q + 1, lanes]

    row = lax.broadcasted_iota(jnp.int32, (ROWS, LANES), 0) + ((strip - par) * TILE - BASE)
    row = jnp.where(row < 0, row + total_rows, row)
    row = jnp.where(row >= total_rows, row - total_rows, row).astype(jnp.float32)
    cor_ref[...] = 2.0 * (0.3 + 0.4 * ((row + 0.5) / total_rows - 0.5))

    for k in range(DEPTH):
        reach = DEPTH - 1 - k
        tiles = (2 * TILE + 2 * reach + TILE - 1) // TILE
        kind = k % 3
        src, dst = ((state, s1), (s1, s2), (s2, state))[kind]
        evaluate(src, state, dst, cor_ref, BASE - reach, tiles, kind)

    def store(keep_row, send_row):
        for j, ct in enumerate(kept):
            i = worked.index(ct)
            keep[:, :, at(j)] = state[:, i, keep_row : keep_row + TILE, :]
            send[:, :, at(j)] = state[:, i, send_row : send_row + TILE, :]

    @pl.when(par == 0)
    def _():
        store(BASE, BASE + TILE)

    @pl.when(par == 1)
    def _():
        store(BASE + TILE, BASE)

    total = jnp.zeros((TILE, LANES), jnp.float32)
    for side in range(2):
        mine = par == side
        obs = [jnp.where(mine, obs_own[k], obs_got[k]) for k in range(3)]
        where = obs[1].astype(jnp.int32)
        tile, lane = where // LANES, where % LANES
        picked = jnp.zeros((TILE, LANES), jnp.float32)
        here = jnp.zeros((TILE, LANES), jnp.bool_)
        for ct in kept:
            i = worked.index(ct)
            eta = state[0, i, BASE + side * TILE : BASE + (side + 1) * TILE, :]
            found = tile == ct
            picked = jnp.where(found, jnp.take_along_axis(eta, lane, axis=1), picked)
            here = here | found
        gap = obs[0] - picked
        total = total + jnp.where(here, obs[2] * gap * gap, 0.0)
    at_slot = lax.broadcasted_iota(jnp.int32, (TILE, LANES), 0) == par * (slots // 2) + slot
    misfit[...] = jnp.where(at_slot, jnp.sum(total), 0.0)


def forecast(own, got, low, high, obs_own, obs_got, piece, ncol, slot, slots, total_rows):
    parts = halves(ncol)
    sent, worked, kept = parts[piece]
    place = []
    for ct in worked:
        p = 0 if ct in parts[0][0] else 1
        place.append((p, parts[p][0].index(ct)))
    block = jax.ShapeDtypeStruct((3, TILE, len(kept) * LANES), own.dtype)
    field = pltpu.VMEM((3, len(worked), ROWS, LANES), jnp.float32)
    args = [own, *got, *low, *high, obs_own, obs_got]
    return pl.pallas_call(
        functools.partial(
            forecast_kernel,
            worked=worked,
            kept=kept,
            ncol=ncol,
            place=place,
            total_rows=total_rows,
            slot=slot,
            slots=slots,
        ),
        out_shape=[block, block, jax.ShapeDtypeStruct((TILE, LANES), jnp.float32)],
        in_specs=[VMEM] * len(args),
        out_specs=[VMEM] * 3,
        scratch_shapes=[field, field, field, pltpu.VMEM((ROWS, LANES), jnp.float32)],
        compiler_params=pltpu.CompilerParams(vmem_limit_bytes=24 * 2**20),
        cost_estimate=cost(7.0),
    )(*args)


def gather_kernel(*refs, ncol):
    out = refs[-1]
    parts = halves(ncol)
    half = out.shape[0] // 2
    par = lax.axis_index("strip") % 2
    n = len(parts)
    for k in range(half):
        for p, (_, _, kept) in enumerate(parts):
            mine, theirs = refs[k * n + p], refs[half * n + k * n + p]
            for j, ct in enumerate(kept):
                out[par * half + k, :, :, at(ct)] = mine[:, :, at(j)]
                out[(1 - par) * half + k, :, :, at(ct)] = theirs[:, :, at(j)]


def gather(keeps, backs, ncol):
    pieces = [x for k in keeps for x in k] + [x for k in backs for x in k]
    return pl.pallas_call(
        functools.partial(gather_kernel, ncol=ncol),
        out_shape=jax.ShapeDtypeStruct((2 * len(keeps), 3, TILE, ncol * LANES), jnp.float32),
        in_specs=[VMEM] * len(pieces),
        out_specs=VMEM,
    )(*pieces)


def local(ensemble, offspring, observations, obs_cols, obs_precision):
    members, _, strip_rows, cols = ensemble.shape
    strips = lax.axis_size("strip")
    total_rows = strips * strip_rows
    strip = lax.axis_index("strip")
    half = members // 2
    ncol = cols // LANES
    parts = halves(ncol)
    swap = [(i, i ^ 1) for i in range(strips)]
    up = [(i, (i + 2) % strips) for i in range(strips)]
    down = [(b, a) for a, b in up]

    leaving, index = leave(offspring, ensemble)
    arrived = lax.ppermute(leaving, "particle", [(0, 1), (1, 0)])
    spans = [(sent[0] * LANES, len(sent) * LANES) for sent, _, _ in parts]
    kept, given = pick(index, ensemble, arrived, spans)

    got = [[lax.ppermute(g, "strip", swap) for g in slot] for slot in given]

    rows = (strip * strip_rows + jnp.arange(strip_rows, dtype=jnp.int32)).astype(jnp.float32)
    weight = obs_precision * (1.0 + 2.0 * (rows + 0.5) / total_rows)[:, None]
    obs_own = jnp.stack([observations, obs_cols.astype(jnp.float32), weight])
    obs_got = lax.ppermute(obs_own, "strip", swap)

    keeps, backs, total = [], [], None
    for k in range(half):
        low, high = [], []
        keeps.append([])
        backs.append([])
        for p, (sent, _, _) in enumerate(parts):
            rising, falling = pack(kept[k], got[k][p], sent)
            low.append(lax.ppermute(rising, "strip", up))
            high.append(lax.ppermute(falling, "strip", down))
            keep, send, misfit = forecast(
                kept[k], got[k][: p + 1], low, high, obs_own, obs_got, p, ncol, k, members, total_rows
            )
            keeps[k].append(keep)
            backs[k].append(lax.ppermute(send, "strip", swap))
            total = misfit if total is None else total + misfit
    step = 1
    while step < strips:
        total = total + lax.ppermute(total, "strip", [(i, i ^ step) for i in range(strips)])
        step *= 2
    state = gather(keeps, backs, ncol)
    log_weights = (-0.5 / (total_rows * obs_cols.shape[1])) * total[:members, 0]
    return (state, log_weights)


def solution(mesh):
    in_specs = (
        P(("group", "particle"), None, "strip", None),
        P("group"),
        P(("group", "strip"), None),
        P(("group", "strip"), None),
        P(("group", "strip"), None),
    )
    out_specs = (P(("group", "particle"), None, "strip", None), P(("group", "particle")))
    return jax.shard_map(local, mesh=mesh, in_specs=in_specs, out_specs=out_specs, check_vma=False)
```

```python
import functools

import jax
import jax.numpy as jnp
from jax import lax
from jax.experimental import pallas as pl
from jax.experimental.pallas import tpu as pltpu
from jax.sharding import PartitionSpec as P

STEPS = 3
DT = 0.4
HALF = 0.5 * DT
DEPTH = 3 * STEPS
LANES = 128
TILE = 8
BASE = 16
ROWS = 48

VMEM = pl.BlockSpec(memory_space=pltpu.VMEM)
SMEM = pl.BlockSpec(memory_space=pltpu.SMEM)
ANY = pl.BlockSpec(memory_space=pl.ANY)


def cost(us):
    return pl.CostEstimate(flops=0, bytes_accessed=int(us * 3.0e6), transcendentals=0)


def plan(ncol, slot, slots):
    every = list(range(ncol))
    if slot < slots - 1:
        return ((every, every, every),)
    cut = ncol // 2 + 2
    return (
        (every[:cut], every[:cut], every[1 : cut - 1]),
        (every[cut:], every[cut - 2 :] + [0, 1], every[cut - 1 :] + [0]),
    )


def at(i):
    return slice(i * LANES, (i + 1) * LANES)


def index_kernel(offspring, index):
    members = index.shape[0]
    here = lax.axis_index("particle")
    cumulative = []
    for i in range(offspring.shape[0]):
        cumulative.append(offspring[i] + (cumulative[-1] if i else 0))
    for k in range(members):
        j = here * members + k
        s = sum((c <= j).astype(jnp.int32) for c in cumulative)
        own = s - here * members
        other = s - (1 - here) * members
        inside = (own >= 0) & (own < members)
        index[k] = jnp.clip(jnp.where(inside, own, members + other), 0, 2 * members - 1)


def sources(offspring, members):
    return pl.pallas_call(
        index_kernel,
        out_shape=jax.ShapeDtypeStruct((members,), jnp.int32),
        in_specs=[SMEM],
        out_specs=SMEM,
    )(offspring)


def fetch(index, slot, own, other, spans, outs, sems):
    members = own.shape[0]
    i = index[slot]

    @pl.when(i < members)
    def _():
        for n, (first, count) in enumerate(spans):
            pltpu.make_async_copy(
                own.at[jnp.minimum(i, members - 1), :, :, pl.ds(first, count)], outs[n], sems.at[n]
            ).start()

    @pl.when(i >= members)
    def _():
        for n, (first, count) in enumerate(spans):
            pltpu.make_async_copy(
                other.at[jnp.maximum(i - members, 0), :, :, pl.ds(first, count)], outs[n], sems.at[n]
            ).start()


def arrive(own, spans, outs, sems):
    for n, (first, count) in enumerate(spans):
        pltpu.make_async_copy(own.at[0, :, :, pl.ds(first, count)], outs[n], sems.at[n]).wait()


def pick_kernel(index, own, other, *refs, slot, spans, before):
    n = len(spans)
    members = own.shape[0]
    half = members // 2
    par = lax.axis_index("strip") % 2
    earlier, refs = refs[: 2 * before], refs[2 * before :]
    kept, given, refs = refs[:n], refs[n : 2 * n], refs[2 * n :]
    sems = refs[-1]
    fetch(index, (1 - par) * half + slot, own, other, spans, given, sems.at[0])
    fetch(index, par * half + slot, own, other, spans, kept, sems.at[1])
    arrive(own, spans, given, sems.at[0])
    arrive(own, spans, kept, sems.at[1])
    if slot < half - 1:
        return
    near, far = refs[0], refs[1]
    ncol = own.shape[3] // LANES
    per = ncol // 4

    def edges(row):
        for ref, blocks, these in (
            (near, earlier[:before], kept),
            (far, earlier[before:], given),
        ):
            for k in range(half):
                for f in range(3):
                    for ct in range(ncol):
                        if k < before:
                            block, j = blocks[k], ct
                        else:
                            m = 0
                            while ct * LANES >= spans[m][0] + spans[m][1]:
                                m += 1
                            block, j = these[m], ct - spans[m][0] // LANES
                        q = (k * 3 + f) * 4 + ct // per
                        ref[q : q + 1, at(ct % per)] = block[f, row : row + 1, at(j)]

    @pl.when(par == 0)
    def _():
        edges(TILE - 1)

    @pl.when(par == 1)
    def _():
        edges(0)


def pick(index, own, other, slot, slots, spans, earlier):
    shape, kind = own.shape[1:3], own.dtype
    outs = [jax.ShapeDtypeStruct(shape + (c,), kind) for _, c in spans] * 2
    if slot == slots - 1:
        outs += [jax.ShapeDtypeStruct((12 * slots, own.shape[3] // 4), kind)] * 2
    return pl.pallas_call(
        functools.partial(pick_kernel, slot=slot, spans=spans, before=len(earlier) // 2),
        out_shape=outs,
        in_specs=[SMEM, ANY, ANY] + [VMEM] * len(earlier),
        out_specs=[VMEM] * len(outs),
        scratch_shapes=[pltpu.SemaphoreType.DMA((2, len(spans)))],
    )(index, own, other, *earlier)


def evaluate(src, state, dst, cor_ref, start, tiles, kind):
    ncol = src.shape[1]
    lane = lax.broadcasted_iota(jnp.int32, (TILE, LANES), 1)
    first = lane == 0
    last = lane == LANES - 1

    def body(t, carry):
        r0 = start + t * TILE
        rows = pl.ds(r0, TILE)
        cor = cor_ref[rows, :]
        for ct in range(ncol):
            mid, around = [], []
            for f in range(3):
                c = src[f, ct, rows, :]
                e = pltpu.roll(
                    jnp.where(first, src[f, (ct + 1) % ncol, rows, :], c), LANES - 1, 1
                )
                w = pltpu.roll(jnp.where(last, src[f, (ct - 1) % ncol, rows, :], c), 1, 1)
                n = src[f, ct, pl.ds(r0 + 1, TILE), :]
                s = src[f, ct, pl.ds(r0 - 1, TILE), :]
                mid.append(c)
                around.append((e, w, n, s))
            eta, u, v = mid
            (eE, eW, eN, eS), (uE, uW, uN, uS), (vE, vW, vN, vS) = around
            duy = uN - uS
            dvx = vE - vW
            dux = uE - uW
            dvy = vN - vS
            flow = (dux + dvy) + ((eE * uE - eW * uW) + (eN * vN - eS * vS))
            lu = v * (cor - duy) - u * dux - (eE - eW)
            lv = u * (cor + dvx) + v * dvy + (eN - eS)
            change = (-flow, lu, -lv)
            for f in range(3):
                if kind == 0:
                    new = mid[f] + HALF * change[f]
                elif kind == 1:
                    new = 0.75 * state[f, ct, rows, :] + (0.25 * mid[f] + (0.25 * HALF) * change[f])
                else:
                    new = (1.0 / 3.0) * state[f, ct, rows, :] + (
                        (2.0 / 3.0) * mid[f] + (2.0 / 3.0 * HALF) * change[f]
                    )
                dst[f, ct, rows, :] = new
        return carry

    lax.fori_loop(0, tiles, body, 0)


def forecast_kernel(*refs, worked, kept, place, parts, slot, slots, ncol, total_rows):
    own, got, direct, passed = (refs[n * parts : (n + 1) * parts] for n in range(4))
    near, far, obs_own, obs_got, keep, send, misfit, state, s1, s2, cor_ref = refs[4 * parts :]
    strip = lax.axis_index("strip")
    par = strip % 2
    per = ncol // 4

    def load(own_row, got_row, direct_row, passed_row, near_row, far_row):
        for i, ct in enumerate(worked):
            p, j = place[i]
            for ref, row in (
                (own, own_row),
                (got, got_row),
                (direct, direct_row),
                (passed, passed_row),
            ):
                state[:, i, row : row + TILE, :] = ref[p][:, :, at(j)]
            for ref, row in ((near, near_row), (far, far_row)):
                for f in range(3):
                    q = (slot * 3 + f) * 4 + ct // per
                    state[f, i, row : row + 1, :] = ref[q : q + 1, at(ct % per)]

    above, below = BASE - TILE, BASE + 2 * TILE

    @pl.when(par == 0)
    def _():
        load(BASE, BASE + TILE, below, above, above - 1, below + TILE)

    @pl.when(par == 1)
    def _():
        load(BASE + TILE, BASE, above, below, below + TILE, above - 1)

    row = lax.broadcasted_iota(jnp.int32, (ROWS, LANES), 0) + ((strip - par) * TILE - BASE)
    row = jnp.where(row < 0, row + total_rows, row)
    row = jnp.where(row >= total_rows, row - total_rows, row).astype(jnp.float32)
    cor_ref[...] = 2.0 * (0.3 + 0.4 * ((row + 0.5) / total_rows - 0.5))

    for k in range(DEPTH):
        reach = DEPTH - 1 - k
        tiles = (2 * TILE + 2 * reach + TILE - 1) // TILE
        kind = k % 3
        src, dst = ((state, s1), (s1, s2), (s2, state))[kind]
        evaluate(src, state, dst, cor_ref, BASE - reach, tiles, kind)

    def store(keep_row, send_row):
        for j, ct in enumerate(kept):
            i = worked.index(ct)
            keep[:, :, at(j)] = state[:, i, keep_row : keep_row + TILE, :]
            send[:, :, at(j)] = state[:, i, send_row : send_row + TILE, :]

    @pl.when(par == 0)
    def _():
        store(BASE, BASE + TILE)

    @pl.when(par == 1)
    def _():
        store(BASE + TILE, BASE)

    total = jnp.zeros((TILE, LANES), jnp.float32)
    for side in range(2):
        mine = par == side
        obs = [jnp.where(mine, obs_own[k], obs_got[k]) for k in range(3)]
        where = obs[1].astype(jnp.int32)
        tile, lane = where // LANES, where % LANES
        picked = jnp.zeros((TILE, LANES), jnp.float32)
        here = jnp.zeros((TILE, LANES), jnp.bool_)
        for ct in kept:
            i = worked.index(ct)
            eta = state[0, i, BASE + side * TILE : BASE + (side + 1) * TILE, :]
            found = tile == ct
            picked = jnp.where(found, jnp.take_along_axis(eta, lane, axis=1), picked)
            here = here | found
        gap = obs[0] - picked
        total = total + jnp.where(here, obs[2] * gap * gap, 0.0)
    at_slot = lax.broadcasted_iota(jnp.int32, (TILE, LANES), 0) == par * slots + slot
    misfit[...] = jnp.where(at_slot, jnp.sum(total), 0.0)


def forecast(own, got, direct, passed, near, far, obs_own, obs_got, piece, slot, slots, ncol, total_rows):
    parts = plan(ncol, slot, slots)
    _, worked, kept = parts[piece]
    place = []
    for ct in worked:
        p = 0 if ct in parts[0][0] else 1
        place.append((p, parts[p][0].index(ct)))
    block = jax.ShapeDtypeStruct((3, TILE, len(kept) * LANES), jnp.float32)
    field = pltpu.VMEM((3, len(worked), ROWS, LANES), jnp.float32)
    args = [*own, *got, *direct, *passed, near, far, obs_own, obs_got]
    return pl.pallas_call(
        functools.partial(
            forecast_kernel,
            worked=worked,
            kept=kept,
            place=place,
            parts=len(own),
            slot=slot,
            slots=slots,
            ncol=ncol,
            total_rows=total_rows,
        ),
        out_shape=[block, block, jax.ShapeDtypeStruct((TILE, LANES), jnp.float32)],
        in_specs=[VMEM] * len(args),
        out_specs=[VMEM] * 3,
        scratch_shapes=[field, field, field, pltpu.VMEM((ROWS, LANES), jnp.float32)],
        compiler_params=pltpu.CompilerParams(vmem_limit_bytes=24 * 2**20),
        cost_estimate=cost(7.0 * len(worked) / 18),
    )(*args)


def gather_kernel(*refs, ncol, slots, pieces):
    out = refs[-1]
    par = lax.axis_index("strip") % 2
    for n, (k, p) in enumerate(pieces):
        mine, theirs = refs[2 * n], refs[2 * n + 1]
        for j, ct in enumerate(plan(ncol, k, slots)[p][2]):
            out[par * slots + k, :, :, at(ct)] = mine[:, :, at(j)]
            out[(1 - par) * slots + k, :, :, at(ct)] = theirs[:, :, at(j)]


def gather(blocks, pieces, ncol, slots):
    args = [b for pair in blocks for b in pair]
    return pl.pallas_call(
        functools.partial(gather_kernel, ncol=ncol, slots=slots, pieces=pieces),
        out_shape=jax.ShapeDtypeStruct((2 * slots, 3, TILE, ncol * LANES), jnp.float32),
        in_specs=[VMEM] * len(args),
        out_specs=VMEM,
    )(*args)


def finish_kernel(before, mine, theirs, out, sems, *, runs, slot, slots):
    par = lax.axis_index("strip") % 2
    copies = []
    for n, (first, start, count) in enumerate(runs):
        for m, (ref, row) in enumerate(
            ((mine, par * slots + slot), (theirs, (1 - par) * slots + slot))
        ):
            copies.append(
                pltpu.make_async_copy(
                    ref.at[:, :, pl.ds(first * LANES, count * LANES)],
                    out.at[row, :, :, pl.ds(start * LANES, count * LANES)],
                    sems.at[2 * n + m],
                )
            )
    for c in copies:
        c.start()
    for c in copies:
        c.wait()


def finish(before, mine, theirs, slot, slots, piece, ncol):
    kept = plan(ncol, slot, slots)[piece][2]
    runs = []
    for j, ct in enumerate(kept):
        if j and ct == kept[j - 1] + 1:
            first, start, count = runs[-1]
            runs[-1] = (first, start, count + 1)
        else:
            runs.append((j, ct, 1))
    return pl.pallas_call(
        functools.partial(finish_kernel, runs=runs, slot=slot, slots=slots),
        out_shape=jax.ShapeDtypeStruct(before.shape, before.dtype),
        in_specs=[ANY, VMEM, VMEM],
        out_specs=ANY,
        scratch_shapes=[pltpu.SemaphoreType.DMA((2 * len(runs),))],
        input_output_aliases={0: 0},
    )(before, mine, theirs)


def local(ensemble, offspring, observations, obs_cols, obs_precision):
    members, _, strip_rows, cols = ensemble.shape
    strips = lax.axis_size("strip")
    total_rows = strips * strip_rows
    strip = lax.axis_index("strip")
    half = members // 2
    ncol = cols // LANES

    def moved(even, odd):
        return [(i, (i + (odd if i % 2 else even)) % strips) for i in range(strips)]

    swap = moved(1, -1)
    straight = moved(-2, 2)
    onward = moved(2, -2)
    cross = moved(3, -3)

    arrived = lax.ppermute(ensemble, "particle", [(0, 1), (1, 0)])
    index = sources(offspring, members)

    rows = (strip * strip_rows + jnp.arange(strip_rows, dtype=jnp.int32)).astype(jnp.float32)
    weight = obs_precision * (1.0 + 2.0 * (rows + 0.5) / total_rows)[:, None]
    obs_own = jnp.stack([observations, obs_cols.astype(jnp.float32), weight])

    kept, given, got, direct, passed = [], [], [], [], []
    earlier = []
    for k in range(half):
        parts = plan(ncol, k, half)
        spans = [(sent[0] * LANES, len(sent) * LANES) for sent, _, _ in parts]
        out = pick(index, ensemble, arrived, k, half, spans, [e[0] for e in kept + given])
        n = len(parts)
        kept.append(out[:n])
        given.append(out[n : 2 * n])
        rest = out[2 * n :]
    near = lax.ppermute(rest[0], "strip", onward)
    far = lax.ppermute(rest[1], "strip", cross)
    for k in range(half):
        got.append([lax.ppermute(g, "strip", swap) for g in given[k]])
        direct.append([lax.ppermute(b, "strip", straight) for b in kept[k]])
        passed.append([lax.ppermute(g, "strip", onward) for g in got[k]])
    obs_got = lax.ppermute(obs_own, "strip", swap)

    blocks, pieces, total = [], [], None
    for k in range(half):
        for p in range(len(plan(ncol, k, half))):
            keep, send, misfit = forecast(
                kept[k][: p + 1],
                got[k][: p + 1],
                direct[k][: p + 1],
                passed[k][: p + 1],
                near,
                far,
                obs_own,
                obs_got,
                p,
                k,
                half,
                ncol,
                total_rows,
            )
            blocks.append((keep, lax.ppermute(send, "strip", swap)))
            pieces.append((k, p))
            total = misfit if total is None else total + misfit
    step = 2
    while step < strips:
        total = total + lax.ppermute(total, "strip", [(i, i ^ step) for i in range(strips)])
        step *= 2
    total = total + lax.ppermute(total, "strip", swap)
    state = gather(blocks[:-1], pieces[:-1], ncol, half)
    state = finish(state, *blocks[-1], half - 1, half, pieces[-1][1], ncol)
    log_weights = (-0.5 / (total_rows * obs_cols.shape[1])) * total[:members, 0]
    return (state, log_weights)


def solution(mesh):
    in_specs = (
        P(("group", "particle"), None, "strip", None),
        P("group"),
        P(("group", "strip"), None),
        P(("group", "strip"), None),
        P(("group", "strip"), None),
    )
    out_specs = (P(("group", "particle"), None, "strip", None), P(("group", "particle")))
    return jax.shard_map(local, mesh=mesh, in_specs=in_specs, out_specs=out_specs, check_vma=False)
```

```python
import functools

import jax
import jax.numpy as jnp
from jax import lax
from jax.experimental import pallas as pl
from jax.experimental.pallas import tpu as pltpu
from jax.sharding import PartitionSpec as P

STEPS = 3
DT = 0.4
HALF = 0.5 * DT
DEPTH = 3 * STEPS
LANES = 128
TILE = 8
BASE = 16
ROWS = 48
SMALL = 12 * 2**20
WORK = 0.005

VMEM = pl.BlockSpec(memory_space=pltpu.VMEM)
SMEM = pl.BlockSpec(memory_space=pltpu.SMEM)
ANY = pl.BlockSpec(memory_space=pl.ANY)


def cost(us):
    return pl.CostEstimate(flops=0, bytes_accessed=int(us * 3.0e6), transcendentals=0)


def plan(ncol, slot, slots):
    every = list(range(ncol))
    if slot < slots - 1:
        return ((every, every, every),)
    cut = ncol // 2 + 2
    return (
        (every[:cut], every[:cut], every[1 : cut - 1]),
        (every[cut:], every[cut - 2 :] + [0, 1], every[cut - 1 :] + [0]),
    )


def after(arrays, first):
    return lax.optimization_barrier((tuple(arrays), first))[0]


def at(i):
    return slice(i * LANES, (i + 1) * LANES)


def index_kernel(offspring, index):
    members = index.shape[0]
    here = lax.axis_index("particle")
    cumulative = []
    for i in range(offspring.shape[0]):
        cumulative.append(offspring[i] + (cumulative[-1] if i else 0))
    for k in range(members):
        j = here * members + k
        s = sum((c <= j).astype(jnp.int32) for c in cumulative)
        own = s - here * members
        other = s - (1 - here) * members
        inside = (own >= 0) & (own < members)
        index[k] = jnp.clip(jnp.where(inside, own, members + other), 0, 2 * members - 1)


def sources(offspring, members):
    return pl.pallas_call(
        index_kernel,
        out_shape=jax.ShapeDtypeStruct((members,), jnp.int32),
        in_specs=[SMEM],
        out_specs=SMEM,
    )(offspring)


def pick_kernel(index, own, other, *outs, spans):
    members = own.shape[0]
    half = members // 2
    par = lax.axis_index("strip") % 2
    refs, kept, given = list(outs), [], []
    for s in spans:
        kept.append([refs.pop(0) for _ in s])
        given.append([refs.pop(0) for _ in s])
    near, far = refs
    wide = own.shape[3] // TILE

    def copy(slot, k, pieces, edge):
        i = index[slot]

        def write(ref, m):
            for (first, count), out in zip(spans[k], pieces):
                out[...] = ref[m, :, :, pl.ds(first, count)]

            def edges(row):
                for f in range(3):
                    for q in range(TILE):
                        edge[k * 3 + f, q : q + 1, :] = ref[
                            m, f, row : row + 1, q * wide : (q + 1) * wide
                        ]

            @pl.when(par == 0)
            def _():
                edges(TILE - 1)

            @pl.when(par == 1)
            def _():
                edges(0)

        @pl.when(i < members)
        def _():
            write(own, jnp.minimum(i, members - 1))

        @pl.when(i >= members)
        def _():
            write(other, jnp.maximum(i - members, 0))

    for k in range(half):
        copy((1 - par) * half + k, k, given[k], far)
        copy(par * half + k, k, kept[k], near)


def pick(index, own, other, spans):
    shape, kind = own.shape[1:3], own.dtype
    outs = []
    for s in spans:
        outs += [jax.ShapeDtypeStruct(shape + (c,), kind) for _, c in s] * 2
    outs += [jax.ShapeDtypeStruct((3 * len(spans), TILE, own.shape[3] // TILE), kind)] * 2
    out = pl.pallas_call(
        functools.partial(pick_kernel, spans=spans),
        out_shape=outs,
        in_specs=[SMEM, VMEM, VMEM],
        out_specs=[VMEM] * len(outs),
        compiler_params=pltpu.CompilerParams(vmem_limit_bytes=SMALL),
    )(index, own, other)
    kept, given = [], []
    for s in spans:
        kept.append(out[: len(s)])
        given.append(out[len(s) : 2 * len(s)])
        out = out[2 * len(s) :]
    return kept, given, out[0], out[1]


def evaluate(src, state, dst, cor_ref, start, tiles, kind):
    ncol = src.shape[1]
    lane = lax.broadcasted_iota(jnp.int32, (TILE, LANES), 1)
    first = lane == 0
    last = lane == LANES - 1

    def body(t, carry):
        r0 = start + t * TILE
        rows = pl.ds(r0, TILE)
        cor = cor_ref[rows, :]
        for ct in range(ncol):
            mid, around = [], []
            for f in range(3):
                c = src[f, ct, rows, :]
                e = pltpu.roll(
                    jnp.where(first, src[f, (ct + 1) % ncol, rows, :], c), LANES - 1, 1
                )
                w = pltpu.roll(jnp.where(last, src[f, (ct - 1) % ncol, rows, :], c), 1, 1)
                n = src[f, ct, pl.ds(r0 + 1, TILE), :]
                s = src[f, ct, pl.ds(r0 - 1, TILE), :]
                mid.append(c)
                around.append((e, w, n, s))
            eta, u, v = mid
            (eE, eW, eN, eS), (uE, uW, uN, uS), (vE, vW, vN, vS) = around
            duy = uN - uS
            dvx = vE - vW
            dux = uE - uW
            dvy = vN - vS
            flow = (dux + dvy) + ((eE * uE - eW * uW) + (eN * vN - eS * vS))
            lu = v * (cor - duy) - u * dux - (eE - eW)
            lv = u * (cor + dvx) + v * dvy + (eN - eS)
            change = (-flow, lu, -lv)
            for f in range(3):
                if kind == 0:
                    new = mid[f] + HALF * change[f]
                elif kind == 1:
                    new = 0.75 * state[f, ct, rows, :] + (0.25 * mid[f] + (0.25 * HALF) * change[f])
                else:
                    new = (1.0 / 3.0) * state[f, ct, rows, :] + (
                        (2.0 / 3.0) * mid[f] + (2.0 / 3.0 * HALF) * change[f]
                    )
                dst[f, ct, rows, :] = new
        return carry

    lax.fori_loop(0, tiles, body, 0)


def forecast_kernel(*refs, worked, kept, place, parts, slot, slots, ncol, total_rows):
    own, got, direct, passed = (refs[n * parts : (n + 1) * parts] for n in range(4))
    near, far, obs_own, obs_got, keep, send, misfit, state, s1, s2, cor_ref = refs[4 * parts :]
    strip = lax.axis_index("strip")
    par = strip % 2
    per = ncol // TILE

    def load(own_row, got_row, direct_row, passed_row, near_row, far_row):
        for i, ct in enumerate(worked):
            p, j = place[i]
            for ref, row in (
                (own, own_row),
                (got, got_row),
                (direct, direct_row),
                (passed, passed_row),
            ):
                state[:, i, row : row + TILE, :] = ref[p][:, :, at(j)]
            for ref, row in ((near, near_row), (far, far_row)):
                q = ct // per
                state[:, i, row : row + 1, :] = ref[
                    slot * 3 : slot * 3 + 3, q : q + 1, at(ct % per)
                ]

    above, below = BASE - TILE, BASE + 2 * TILE

    @pl.when(par == 0)
    def _():
        load(BASE, BASE + TILE, below, above, above - 1, below + TILE)

    @pl.when(par == 1)
    def _():
        load(BASE + TILE, BASE, above, below, below + TILE, above - 1)

    row = lax.broadcasted_iota(jnp.int32, (ROWS, LANES), 0) + ((strip - par) * TILE - BASE)
    row = jnp.where(row < 0, row + total_rows, row)
    row = jnp.where(row >= total_rows, row - total_rows, row).astype(jnp.float32)
    cor_ref[...] = 2.0 * (0.3 + 0.4 * ((row + 0.5) / total_rows - 0.5))

    for k in range(DEPTH):
        reach = DEPTH - 1 - k
        tiles = (2 * TILE + 2 * reach + TILE - 1) // TILE
        kind = k % 3
        src, dst = ((state, s1), (s1, s2), (s2, state))[kind]
        evaluate(src, state, dst, cor_ref, BASE - reach, tiles, kind)

    def store(keep_row, send_row):
        for j, ct in enumerate(kept):
            i = worked.index(ct)
            keep[:, :, at(j)] = state[:, i, keep_row : keep_row + TILE, :]
            send[:, :, at(j)] = state[:, i, send_row : send_row + TILE, :]

    @pl.when(par == 0)
    def _():
        store(BASE, BASE + TILE)

    @pl.when(par == 1)
    def _():
        store(BASE + TILE, BASE)

    total = jnp.zeros((TILE, LANES), jnp.float32)
    for side in range(2):
        mine = par == side
        obs = [jnp.where(mine, obs_own[k], obs_got[k]) for k in range(3)]
        where = obs[1].astype(jnp.int32)
        tile, lane = where // LANES, where % LANES
        picked = jnp.zeros((TILE, LANES), jnp.float32)
        here = jnp.zeros((TILE, LANES), jnp.bool_)
        for ct in kept:
            i = worked.index(ct)
            eta = state[0, i, BASE + side * TILE : BASE + (side + 1) * TILE, :]
            found = tile == ct
            picked = jnp.where(found, jnp.take_along_axis(eta, lane, axis=1), picked)
            here = here | found
        gap = obs[0] - picked
        total = total + jnp.where(here, obs[2] * gap * gap, 0.0)
    at_slot = lax.broadcasted_iota(jnp.int32, (TILE, LANES), 0) == par * slots + slot
    misfit[...] = jnp.where(at_slot, jnp.sum(total), 0.0)


def forecast(own, got, direct, passed, near, far, obs_own, obs_got, piece, slot, slots, ncol, total_rows):
    parts = plan(ncol, slot, slots)
    _, worked, kept = parts[piece]
    place = []
    for ct in worked:
        p = 0 if ct in parts[0][0] else 1
        place.append((p, parts[p][0].index(ct)))
    block = jax.ShapeDtypeStruct((3, TILE, len(kept) * LANES), jnp.float32)
    field = pltpu.VMEM((3, len(worked), ROWS, LANES), jnp.float32)
    args = [*own, *got, *direct, *passed, near, far, obs_own, obs_got]
    return pl.pallas_call(
        functools.partial(
            forecast_kernel,
            worked=worked,
            kept=kept,
            place=place,
            parts=len(own),
            slot=slot,
            slots=slots,
            ncol=ncol,
            total_rows=total_rows,
        ),
        out_shape=[block, block, jax.ShapeDtypeStruct((TILE, LANES), jnp.float32)],
        in_specs=[VMEM] * len(args),
        out_specs=[VMEM] * 3,
        scratch_shapes=[field, field, field, pltpu.VMEM((ROWS, LANES), jnp.float32)],
        compiler_params=pltpu.CompilerParams(vmem_limit_bytes=24 * 2**20),
        cost_estimate=cost(WORK * len(worked)),
    )(*args)


def gather_kernel(*refs, ncol, slots, pieces):
    out = refs[-1]
    par = lax.axis_index("strip") % 2
    for n, (k, p) in enumerate(pieces):
        mine, theirs = refs[2 * n], refs[2 * n + 1]
        for j, ct in enumerate(plan(ncol, k, slots)[p][2]):
            out[par * slots + k, :, :, at(ct)] = mine[:, :, at(j)]
            out[(1 - par) * slots + k, :, :, at(ct)] = theirs[:, :, at(j)]


def gather(blocks, pieces, ncol, slots):
    args = [b for pair in blocks for b in pair]
    return pl.pallas_call(
        functools.partial(gather_kernel, ncol=ncol, slots=slots, pieces=pieces),
        out_shape=jax.ShapeDtypeStruct((2 * slots, 3, TILE, ncol * LANES), jnp.float32),
        in_specs=[VMEM] * len(args),
        out_specs=VMEM,
        compiler_params=pltpu.CompilerParams(vmem_limit_bytes=SMALL),
        cost_estimate=cost(0.1),
    )(*args)


def local(ensemble, offspring, observations, obs_cols, obs_precision):
    members, _, strip_rows, cols = ensemble.shape
    strips = lax.axis_size("strip")
    total_rows = strips * strip_rows
    strip = lax.axis_index("strip")
    half = members // 2
    ncol = cols // LANES

    def moved(even, odd):
        return [(i, (i + (odd if i % 2 else even)) % strips) for i in range(strips)]

    swap = moved(1, -1)
    straight = moved(-2, 2)
    onward = moved(2, -2)
    cross = moved(3, -3)

    arrived = lax.ppermute(ensemble, "particle", [(0, 1), (1, 0)])
    index = sources(offspring, members)

    rows = (strip * strip_rows + jnp.arange(strip_rows, dtype=jnp.int32)).astype(jnp.float32)
    weight = obs_precision * (1.0 + 2.0 * (rows + 0.5) / total_rows)[:, None]
    obs_own = jnp.stack([observations, obs_cols.astype(jnp.float32), weight])

    spans = [
        [(sent[0] * LANES, len(sent) * LANES) for sent, _, _ in plan(ncol, k, half)]
        for k in range(half)
    ]
    kept, given, near, far = pick(index, ensemble, arrived, spans)
    near = lax.ppermute(near, "strip", onward)
    far = lax.ppermute(far, "strip", cross)

    got, direct, passed = [], [], []
    swapped = None
    for k in range(half):
        got.append([])
        direct.append([])
        passed.append([])
        for p in range(len(spans[k])):
            giving, keeping = given[k][p], kept[k][p]
            if k > 0:
                (giving,) = after((giving,), swapped)
                (keeping,) = after((keeping,), passed[0][0] if p else (near, far))
            swapped = lax.ppermute(giving, "strip", swap)
            got[k].append(swapped)
            direct[k].append(lax.ppermute(keeping, "strip", straight))
            goes = swapped
            if k == 0:
                (goes,) = after((goes,), direct[0][0])
            elif p > 0:
                (goes,) = after((goes,), passed[0][0])
            passed[k].append(lax.ppermute(goes, "strip", onward))
    obs_got = lax.ppermute(obs_own, "strip", swap)

    obs_got = lax.ppermute(obs_own, "strip", swap)

    obs_got = lax.ppermute(obs_own, "strip", swap)

    blocks, pieces, total = [], [], None
    for k in range(half):
        for p in range(len(plan(ncol, k, half))):
            keep, send, misfit = forecast(
                kept[k][: p + 1],
                got[k][: p + 1],
                direct[k][: p + 1],
                passed[k][: p + 1],
                near,
                far,
                obs_own,
                obs_got,
                p,
                k,
                half,
                ncol,
                total_rows,
            )
            blocks.append((keep, lax.ppermute(send, "strip", swap)))
            pieces.append((k, p))
            total = misfit if total is None else total + misfit
    (total,) = after((total,), [b[1] for b in blocks[:-1]])
    if strips == 8:
        turn = [lax.ppermute(total, "strip", moved(step, step)) for step in (2, 4, 6)]
        total = (total + turn[1]) + (turn[0] + turn[2])
    else:
        step = 2
        while step < strips:
            total = total + lax.ppermute(total, "strip", [(i, i ^ step) for i in range(strips)])
            step *= 2
    total = total + lax.ppermute(total, "strip", swap)
    state = gather(blocks, pieces, ncol, half)
    (total,) = after((total,), state)
    log_weights = (-0.5 / (total_rows * obs_cols.shape[1])) * total[:members, 0]
    return (state, log_weights)


def solution(mesh):
    in_specs = (
        P(("group", "particle"), None, "strip", None),
        P("group"),
        P(("group", "strip"), None),
        P(("group", "strip"), None),
        P(("group", "strip"), None),
    )
    out_specs = (P(("group", "particle"), None, "strip", None), P(("group", "particle")))
    return jax.shard_map(local, mesh=mesh, in_specs=in_specs, out_specs=out_specs, check_vma=False)
```

```python
import functools

import jax
import jax.numpy as jnp
from jax import lax
from jax.experimental import pallas as pl
from jax.experimental.pallas import tpu as pltpu
from jax.sharding import PartitionSpec as P

STEPS = 3
DT = 0.4
HALF = 0.5 * DT
DEPTH = 3 * STEPS
LANES = 128
TILE = 8
BASE = 16
ROWS = 48
SMALL = 12 * 2**20
WORK = 0.005

VMEM = pl.BlockSpec(memory_space=pltpu.VMEM)
SMEM = pl.BlockSpec(memory_space=pltpu.SMEM)
ANY = pl.BlockSpec(memory_space=pl.ANY)


def cost(us):
    return pl.CostEstimate(flops=0, bytes_accessed=int(us * 3.0e6), transcendentals=0)


def plan(ncol, slot, slots):
    every = list(range(ncol))
    if slot < slots - 1:
        return ((every, every, every),)
    cut = ncol // 2 + 2
    return (
        (every[:cut], every[:cut], every[1 : cut - 1]),
        (every[cut:], every[cut - 2 :] + [0, 1], every[cut - 1 :] + [0]),
    )


def after(arrays, first):
    return lax.optimization_barrier((tuple(arrays), first))[0]


def at(i):
    return slice(i * LANES, (i + 1) * LANES)


def index_kernel(offspring, ensemble, index):
    members = index.shape[0]
    here = lax.axis_index("particle")
    cumulative = []
    for i in range(offspring.shape[0]):
        cumulative.append(offspring[i] + (cumulative[-1] if i else 0))
    for k in range(members):
        j = here * members + k
        s = sum((c <= j).astype(jnp.int32) for c in cumulative)
        own = s - here * members
        other = s - (1 - here) * members
        inside = (own >= 0) & (own < members)
        index[k] = jnp.clip(jnp.where(inside, own, members + other), 0, 2 * members - 1)


def sources(offspring, ensemble):
    members = ensemble.shape[0]
    return pl.pallas_call(
        index_kernel,
        out_shape=jax.ShapeDtypeStruct((members,), jnp.int32),
        in_specs=[SMEM, VMEM],
        out_specs=SMEM,
        compiler_params=pltpu.CompilerParams(vmem_limit_bytes=SMALL),
    )(offspring, ensemble)


def pick_kernel(index, own, other, *outs, spans):
    members = own.shape[0]
    half = members // 2
    par = lax.axis_index("strip") % 2
    refs, kept, given = list(outs), [], []
    for s in spans:
        kept.append([refs.pop(0) for _ in s])
        given.append([refs.pop(0) for _ in s])
    near, far = refs
    wide = own.shape[3] // TILE

    def copy(slot, k, pieces, edge):
        i = index[slot]

        def write(ref, m):
            for (first, count), out in zip(spans[k], pieces):
                out[...] = ref[m, :, :, pl.ds(first, count)]

            def edges(row):
                for f in range(3):
                    for q in range(TILE):
                        edge[k * 3 + f, q : q + 1, :] = ref[
                            m, f, row : row + 1, q * wide : (q + 1) * wide
                        ]

            @pl.when(par == 0)
            def _():
                edges(TILE - 1)

            @pl.when(par == 1)
            def _():
                edges(0)

        @pl.when(i < members)
        def _():
            write(own, jnp.minimum(i, members - 1))

        @pl.when(i >= members)
        def _():
            write(other, jnp.maximum(i - members, 0))

    for k in range(half):
        copy((1 - par) * half + k, k, given[k], far)
        copy(par * half + k, k, kept[k], near)


def pick(index, own, other, spans):
    shape, kind = own.shape[1:3], own.dtype
    outs = []
    for s in spans:
        outs += [jax.ShapeDtypeStruct(shape + (c,), kind) for _, c in s] * 2
    outs += [jax.ShapeDtypeStruct((3 * len(spans), TILE, own.shape[3] // TILE), kind)] * 2
    out = pl.pallas_call(
        functools.partial(pick_kernel, spans=spans),
        out_shape=outs,
        in_specs=[SMEM, VMEM, VMEM],
        out_specs=[VMEM] * len(outs),
        compiler_params=pltpu.CompilerParams(vmem_limit_bytes=SMALL),
    )(index, own, other)
    kept, given = [], []
    for s in spans:
        kept.append(out[: len(s)])
        given.append(out[len(s) : 2 * len(s)])
        out = out[2 * len(s) :]
    return kept, given, out[0], out[1]


def evaluate(src, state, dst, cor_ref, start, tiles, kind):
    ncol = src.shape[1]
    lane = lax.broadcasted_iota(jnp.int32, (TILE, LANES), 1)
    first = lane == 0
    last = lane == LANES - 1

    def body(t, carry):
        r0 = start + t * TILE
        rows = pl.ds(r0, TILE)
        cor = cor_ref[rows, :]
        for ct in range(ncol):
            mid, around = [], []
            for f in range(3):
                c = src[f, ct, rows, :]
                e = pltpu.roll(
                    jnp.where(first, src[f, (ct + 1) % ncol, rows, :], c), LANES - 1, 1
                )
                w = pltpu.roll(jnp.where(last, src[f, (ct - 1) % ncol, rows, :], c), 1, 1)
                n = src[f, ct, pl.ds(r0 + 1, TILE), :]
                s = src[f, ct, pl.ds(r0 - 1, TILE), :]
                mid.append(c)
                around.append((e, w, n, s))
            eta, u, v = mid
            (eE, eW, eN, eS), (uE, uW, uN, uS), (vE, vW, vN, vS) = around
            duy = uN - uS
            dvx = vE - vW
            dux = uE - uW
            dvy = vN - vS
            flow = (dux + dvy) + ((eE * uE - eW * uW) + (eN * vN - eS * vS))
            lu = v * (cor - duy) - u * dux - (eE - eW)
            lv = u * (cor + dvx) + v * dvy + (eN - eS)
            change = (-flow, lu, -lv)
            for f in range(3):
                if kind == 0:
                    new = mid[f] + HALF * change[f]
                elif kind == 1:
                    new = 0.75 * state[f, ct, rows, :] + (0.25 * mid[f] + (0.25 * HALF) * change[f])
                else:
                    new = (1.0 / 3.0) * state[f, ct, rows, :] + (
                        (2.0 / 3.0) * mid[f] + (2.0 / 3.0 * HALF) * change[f]
                    )
                dst[f, ct, rows, :] = new
        return carry

    lax.fori_loop(0, tiles, body, 0)


def forecast_kernel(*refs, worked, kept, place, parts, slot, slots, ncol, total_rows):
    own, got, direct, passed = (refs[n * parts : (n + 1) * parts] for n in range(4))
    near, far, obs_own, obs_got, keep, send, misfit, state, s1, s2, cor_ref = refs[4 * parts :]
    strip = lax.axis_index("strip")
    par = strip % 2
    per = ncol // TILE

    def load(own_row, got_row, direct_row, passed_row, near_row, far_row):
        for i, ct in enumerate(worked):
            p, j = place[i]
            for ref, row in (
                (own, own_row),
                (got, got_row),
                (direct, direct_row),
                (passed, passed_row),
            ):
                state[:, i, row : row + TILE, :] = ref[p][:, :, at(j)]
            for ref, row in ((near, near_row), (far, far_row)):
                q = ct // per
                state[:, i, row : row + 1, :] = ref[
                    slot * 3 : slot * 3 + 3, q : q + 1, at(ct % per)
                ]

    above, below = BASE - TILE, BASE + 2 * TILE

    @pl.when(par == 0)
    def _():
        load(BASE, BASE + TILE, below, above, above - 1, below + TILE)

    @pl.when(par == 1)
    def _():
        load(BASE + TILE, BASE, above, below, below + TILE, above - 1)

    row = lax.broadcasted_iota(jnp.int32, (ROWS, LANES), 0) + ((strip - par) * TILE - BASE)
    row = jnp.where(row < 0, row + total_rows, row)
    row = jnp.where(row >= total_rows, row - total_rows, row).astype(jnp.float32)
    cor_ref[...] = 2.0 * (0.3 + 0.4 * ((row + 0.5) / total_rows - 0.5))

    for k in range(DEPTH):
        reach = DEPTH - 1 - k
        tiles = (2 * TILE + 2 * reach + TILE - 1) // TILE
        kind = k % 3
        src, dst = ((state, s1), (s1, s2), (s2, state))[kind]
        evaluate(src, state, dst, cor_ref, BASE - reach, tiles, kind)

    def store(keep_row, send_row):
        for j, ct in enumerate(kept):
            i = worked.index(ct)
            keep[:, :, at(j)] = state[:, i, keep_row : keep_row + TILE, :]
            send[:, :, at(j)] = state[:, i, send_row : send_row + TILE, :]

    @pl.when(par == 0)
    def _():
        store(BASE, BASE + TILE)

    @pl.when(par == 1)
    def _():
        store(BASE + TILE, BASE)

    total = jnp.zeros((TILE, LANES), jnp.float32)
    for side in range(2):
        mine = par == side
        obs = [jnp.where(mine, obs_own[k], obs_got[k]) for k in range(3)]
        where = obs[1].astype(jnp.int32)
        tile, lane = where // LANES, where % LANES
        picked = jnp.zeros((TILE, LANES), jnp.float32)
        here = jnp.zeros((TILE, LANES), jnp.bool_)
        for ct in kept:
            i = worked.index(ct)
            eta = state[0, i, BASE + side * TILE : BASE + (side + 1) * TILE, :]
            found = tile == ct
            picked = jnp.where(found, jnp.take_along_axis(eta, lane, axis=1), picked)
            here = here | found
        gap = obs[0] - picked
        total = total + jnp.where(here, obs[2] * gap * gap, 0.0)
    at_slot = lax.broadcasted_iota(jnp.int32, (TILE, LANES), 1) == par * slots + slot
    misfit[...] = jnp.where(at_slot, jnp.sum(total), 0.0)


def forecast(own, got, direct, passed, near, far, obs_own, obs_got, piece, slot, slots, ncol, total_rows):
    parts = plan(ncol, slot, slots)
    _, worked, kept = parts[piece]
    place = []
    for ct in worked:
        p = 0 if ct in parts[0][0] else 1
        place.append((p, parts[p][0].index(ct)))
    block = jax.ShapeDtypeStruct((3, TILE, len(kept) * LANES), jnp.float32)
    field = pltpu.VMEM((3, len(worked), ROWS, LANES), jnp.float32)
    args = [*own, *got, *direct, *passed, near, far, obs_own, obs_got]
    return pl.pallas_call(
        functools.partial(
            forecast_kernel,
            worked=worked,
            kept=kept,
            place=place,
            parts=len(own),
            slot=slot,
            slots=slots,
            ncol=ncol,
            total_rows=total_rows,
        ),
        out_shape=[block, block, jax.ShapeDtypeStruct((TILE, LANES), jnp.float32)],
        in_specs=[VMEM] * len(args),
        out_specs=[VMEM] * 3,
        scratch_shapes=[field, field, field, pltpu.VMEM((ROWS, LANES), jnp.float32)],
        compiler_params=pltpu.CompilerParams(vmem_limit_bytes=24 * 2**20),
        cost_estimate=cost(WORK * len(worked)),
    )(*args)


def gather_kernel(*refs, ncol, slots, pieces):
    out = refs[-1]
    par = lax.axis_index("strip") % 2
    for n, (k, p) in enumerate(pieces):
        mine, theirs = refs[2 * n], refs[2 * n + 1]
        for j, ct in enumerate(plan(ncol, k, slots)[p][2]):
            out[par * slots + k, :, :, at(ct)] = mine[:, :, at(j)]
            out[(1 - par) * slots + k, :, :, at(ct)] = theirs[:, :, at(j)]


def gather(blocks, pieces, ncol, slots):
    args = [b for pair in blocks for b in pair]
    return pl.pallas_call(
        functools.partial(gather_kernel, ncol=ncol, slots=slots, pieces=pieces),
        out_shape=jax.ShapeDtypeStruct((2 * slots, 3, TILE, ncol * LANES), jnp.float32),
        in_specs=[VMEM] * len(args),
        out_specs=VMEM,
        compiler_params=pltpu.CompilerParams(vmem_limit_bytes=SMALL),
        cost_estimate=cost(0.1),
    )(*args)


def local(ensemble, offspring, observations, obs_cols, obs_precision):
    members, _, strip_rows, cols = ensemble.shape
    strips = lax.axis_size("strip")
    total_rows = strips * strip_rows
    strip = lax.axis_index("strip")
    half = members // 2
    ncol = cols // LANES

    def moved(even, odd):
        return [(i, (i + (odd if i % 2 else even)) % strips) for i in range(strips)]

    swap = moved(1, -1)
    straight = moved(-2, 2)
    onward = moved(2, -2)
    cross = moved(3, -3)

    arrived = lax.ppermute(ensemble, "particle", [(0, 1), (1, 0)])
    index = sources(offspring, ensemble)

    rows = (strip * strip_rows + jnp.arange(strip_rows, dtype=jnp.int32)).astype(jnp.float32)
    weight = obs_precision * (1.0 + 2.0 * (rows + 0.5) / total_rows)[:, None]
    obs_own = jnp.stack([observations, obs_cols.astype(jnp.float32), weight])

    spans = [
        [(sent[0] * LANES, len(sent) * LANES) for sent, _, _ in plan(ncol, k, half)]
        for k in range(half)
    ]
    kept, given, near, far = pick(index, ensemble, arrived, spans)
    near = lax.ppermute(near, "strip", onward)
    far = lax.ppermute(far, "strip", cross)

    got, direct, passed = [], [], []
    swapped, held = None, (near, far)
    for k in range(half):
        got.append([])
        direct.append([])
        passed.append([])
        for p in range(len(spans[k])):
            giving, keeping = given[k][p], kept[k][p]
            if swapped is not None:
                (giving,) = after((giving,), swapped)
            if k > 0 and p > 0:
                (keeping,) = after((keeping,), direct[k][p - 1])
            swapped = lax.ppermute(giving, "strip", swap)
            got[k].append(swapped)
            direct[k].append(lax.ppermute(keeping, "strip", straight))
            (goes,) = after((swapped,), (direct[k][p], held))
            passed[k].append(lax.ppermute(goes, "strip", onward))
            if k > 0:
                held = passed[0][-1]
    obs_got = lax.ppermute(obs_own, "strip", swap)

    obs_got = lax.ppermute(obs_own, "strip", swap)

    obs_got = lax.ppermute(obs_own, "strip", swap)

    obs_got = lax.ppermute(obs_own, "strip", swap)

    blocks, pieces, total = [], [], None
    for k in range(half):
        for p in range(len(plan(ncol, k, half))):
            keep, send, misfit = forecast(
                kept[k][: p + 1],
                got[k][: p + 1],
                direct[k][: p + 1],
                passed[k][: p + 1],
                near,
                far,
                obs_own,
                obs_got,
                p,
                k,
                half,
                ncol,
                total_rows,
            )
            blocks.append((keep, lax.ppermute(send, "strip", swap)))
            pieces.append((k, p))
            total = misfit if total is None else total + misfit
    (total,) = after((total,), [b[1] for b in blocks[:-1]])
    if strips == 8:
        turn = [lax.ppermute(total, "strip", moved(step, step)) for step in (2, 4, 6)]
        total = (total + turn[1]) + (turn[0] + turn[2])
    else:
        step = 2
        while step < strips:
            total = total + lax.ppermute(total, "strip", [(i, i ^ step) for i in range(strips)])
            step *= 2
    total = total + lax.ppermute(total, "strip", swap)
    state = gather(blocks, pieces, ncol, half)
    (total,) = after((total,), state)
    log_weights = (-0.5 / (total_rows * obs_cols.shape[1])) * total[0, :members]
    return (state, log_weights)


def solution(mesh):
    in_specs = (
        P(("group", "particle"), None, "strip", None),
        P("group"),
        P(("group", "strip"), None),
        P(("group", "strip"), None),
        P(("group", "strip"), None),
    )
    out_specs = (P(("group", "particle"), None, "strip", None), P(("group", "particle")))
    return jax.shard_map(local, mesh=mesh, in_specs=in_specs, out_specs=out_specs, check_vma=False)
```

```python
import functools

import jax
import jax.numpy as jnp
from jax import lax
from jax.experimental import pallas as pl
from jax.experimental.pallas import tpu as pltpu
from jax.sharding import PartitionSpec as P

STEPS = 3
DT = 0.4
HALF = 0.5 * DT
DEPTH = 3 * STEPS
LANES = 128
TILE = 8
BASE = 16
ROWS = 48
SMALL = 12 * 2**20
WORK = 0.005

VMEM = pl.BlockSpec(memory_space=pltpu.VMEM)
SMEM = pl.BlockSpec(memory_space=pltpu.SMEM)
ANY = pl.BlockSpec(memory_space=pl.ANY)


def cost(us):
    return pl.CostEstimate(flops=0, bytes_accessed=int(us * 3.0e6), transcendentals=0)


def plan(ncol, slot, slots):
    every = list(range(ncol))
    cut = ncol // 2 + 2
    return (
        (every[:cut], every[:cut], every[1 : cut - 1]),
        (every[cut:], every[cut - 2 :] + [0, 1], every[cut - 1 :] + [0]),
    )


def after(arrays, first):
    return lax.optimization_barrier((tuple(arrays), first))[0]


def at(i):
    return slice(i * LANES, (i + 1) * LANES)


def index_kernel(offspring, ensemble, index):
    members = index.shape[0]
    here = lax.axis_index("particle")
    cumulative = []
    for i in range(offspring.shape[0]):
        cumulative.append(offspring[i] + (cumulative[-1] if i else 0))
    for k in range(members):
        j = here * members + k
        s = sum((c <= j).astype(jnp.int32) for c in cumulative)
        own = s - here * members
        other = s - (1 - here) * members
        inside = (own >= 0) & (own < members)
        index[k] = jnp.clip(jnp.where(inside, own, members + other), 0, 2 * members - 1)


def sources(offspring, ensemble):
    members = ensemble.shape[0]
    return pl.pallas_call(
        index_kernel,
        out_shape=jax.ShapeDtypeStruct((members,), jnp.int32),
        in_specs=[SMEM, VMEM],
        out_specs=SMEM,
        compiler_params=pltpu.CompilerParams(vmem_limit_bytes=SMALL),
    )(offspring, ensemble)


def pick_kernel(index, own, other, *outs, spans):
    members = own.shape[0]
    half = members // 2
    par = lax.axis_index("strip") % 2
    refs, kept, given = list(outs), [], []
    for s in spans:
        kept.append([refs.pop(0)])
        given.append([refs.pop(0) for _ in s])
    near, far = refs
    wide = own.shape[3] // TILE

    def copy(slot, k, pieces, edge):
        i = index[slot]

        def write(ref, m):
            if len(pieces) == 1:
                pieces[0][...] = ref[m]
            else:
                for (first, count), out in zip(spans[k], pieces):
                    out[...] = ref[m, :, :, pl.ds(first, count)]

            def edges(row):
                for f in range(3):
                    for q in range(TILE):
                        edge[k * 3 + f, q : q + 1, :] = ref[
                            m, f, row : row + 1, q * wide : (q + 1) * wide
                        ]

            @pl.when(par == 0)
            def _():
                edges(TILE - 1)

            @pl.when(par == 1)
            def _():
                edges(0)

        @pl.when(i < members)
        def _():
            write(own, jnp.minimum(i, members - 1))

        @pl.when(i >= members)
        def _():
            write(other, jnp.maximum(i - members, 0))

    for k in range(half):
        copy((1 - par) * half + k, k, given[k], far)
        copy(par * half + k, k, kept[k], near)


def pick(index, own, other, spans):
    shape, kind = own.shape[1:3], own.dtype
    outs = []
    for s in spans:
        outs += [jax.ShapeDtypeStruct(shape + (c,), kind) for c in [own.shape[3]] + [c for _, c in s]]
    outs += [jax.ShapeDtypeStruct((3 * len(spans), TILE, own.shape[3] // TILE), kind)] * 2
    out = pl.pallas_call(
        functools.partial(pick_kernel, spans=spans),
        out_shape=outs,
        in_specs=[SMEM, VMEM, VMEM],
        out_specs=[VMEM] * len(outs),
        compiler_params=pltpu.CompilerParams(vmem_limit_bytes=SMALL),
    )(index, own, other)
    kept, given = [], []
    for s in spans:
        kept.append(out[0])
        given.append(out[1 : 1 + len(s)])
        out = out[1 + len(s) :]
    return kept, given, out[0], out[1]


def evaluate(src, state, dst, cor_ref, start, tiles, kind):
    ncol = src.shape[1]
    lane = lax.broadcasted_iota(jnp.int32, (TILE, LANES), 1)
    first = lane == 0
    last = lane == LANES - 1

    def body(t, carry):
        r0 = start + t * TILE
        rows = pl.ds(r0, TILE)
        cor = cor_ref[rows, :]
        for ct in range(ncol):
            mid, around = [], []
            for f in range(3):
                c = src[f, ct, rows, :]
                e = pltpu.roll(
                    jnp.where(first, src[f, (ct + 1) % ncol, rows, :], c), LANES - 1, 1
                )
                w = pltpu.roll(jnp.where(last, src[f, (ct - 1) % ncol, rows, :], c), 1, 1)
                n = src[f, ct, pl.ds(r0 + 1, TILE), :]
                s = src[f, ct, pl.ds(r0 - 1, TILE), :]
                mid.append(c)
                around.append((e, w, n, s))
            eta, u, v = mid
            (eE, eW, eN, eS), (uE, uW, uN, uS), (vE, vW, vN, vS) = around
            duy = uN - uS
            dvx = vE - vW
            dux = uE - uW
            dvy = vN - vS
            flow = (dux + dvy) + ((eE * uE - eW * uW) + (eN * vN - eS * vS))
            lu = v * (cor - duy) - u * dux - (eE - eW)
            lv = u * (cor + dvx) + v * dvy + (eN - eS)
            change = (-flow, lu, -lv)
            for f in range(3):
                if kind == 0:
                    new = mid[f] + HALF * change[f]
                elif kind == 1:
                    new = 0.75 * state[f, ct, rows, :] + (0.25 * mid[f] + (0.25 * HALF) * change[f])
                else:
                    new = (1.0 / 3.0) * state[f, ct, rows, :] + (
                        (2.0 / 3.0) * mid[f] + (2.0 / 3.0 * HALF) * change[f]
                    )
                dst[f, ct, rows, :] = new
        return carry

    lax.fori_loop(0, tiles, body, 0)


def forecast_kernel(*refs, worked, kept, place, parts, slot, slots, ncol, total_rows):
    own, direct, refs = refs[0], refs[1], refs[2:]
    got, passed = refs[:parts], refs[parts : 2 * parts]
    near, far, obs_own, obs_got, keep, send, misfit, state, s1, s2, cor_ref = refs[2 * parts :]
    strip = lax.axis_index("strip")
    par = strip % 2
    per = ncol // TILE

    def load(own_row, got_row, direct_row, passed_row, near_row, far_row):
        for i, ct in enumerate(worked):
            p, j = place[i]
            for ref, row, place_at in (
                (own, own_row, ct),
                (got[p], got_row, j),
                (direct, direct_row, ct),
                (passed[p], passed_row, j),
            ):
                state[:, i, row : row + TILE, :] = ref[:, :, at(place_at)]
            for ref, row in ((near, near_row), (far, far_row)):
                q = ct // per
                state[:, i, row : row + 1, :] = ref[
                    slot * 3 : slot * 3 + 3, q : q + 1, at(ct % per)
                ]

    above, below = BASE - TILE, BASE + 2 * TILE

    @pl.when(par == 0)
    def _():
        load(BASE, BASE + TILE, below, above, above - 1, below + TILE)

    @pl.when(par == 1)
    def _():
        load(BASE + TILE, BASE, above, below, below + TILE, above - 1)

    row = lax.broadcasted_iota(jnp.int32, (ROWS, LANES), 0) + ((strip - par) * TILE - BASE)
    row = jnp.where(row < 0, row + total_rows, row)
    row = jnp.where(row >= total_rows, row - total_rows, row).astype(jnp.float32)
    cor_ref[...] = 2.0 * (0.3 + 0.4 * ((row + 0.5) / total_rows - 0.5))

    for k in range(DEPTH):
        reach = DEPTH - 1 - k
        tiles = (2 * TILE + 2 * reach + TILE - 1) // TILE
        kind = k % 3
        src, dst = ((state, s1), (s1, s2), (s2, state))[kind]
        evaluate(src, state, dst, cor_ref, BASE - reach, tiles, kind)

    def store(keep_row, send_row):
        for j, ct in enumerate(kept):
            i = worked.index(ct)
            keep[:, :, at(j)] = state[:, i, keep_row : keep_row + TILE, :]
            send[:, :, at(j)] = state[:, i, send_row : send_row + TILE, :]

    @pl.when(par == 0)
    def _():
        store(BASE, BASE + TILE)

    @pl.when(par == 1)
    def _():
        store(BASE + TILE, BASE)

    total = jnp.zeros((TILE, LANES), jnp.float32)
    for side in range(2):
        mine = par == side
        obs = [jnp.where(mine, obs_own[k], obs_got[k]) for k in range(3)]
        where = obs[1].astype(jnp.int32)
        tile, lane = where // LANES, where % LANES
        picked = jnp.zeros((TILE, LANES), jnp.float32)
        here = jnp.zeros((TILE, LANES), jnp.bool_)
        for ct in kept:
            i = worked.index(ct)
            eta = state[0, i, BASE + side * TILE : BASE + (side + 1) * TILE, :]
            found = tile == ct
            picked = jnp.where(found, jnp.take_along_axis(eta, lane, axis=1), picked)
            here = here | found
        gap = obs[0] - picked
        total = total + jnp.where(here, obs[2] * gap * gap, 0.0)
    at_slot = lax.broadcasted_iota(jnp.int32, (TILE, LANES), 1) == par * slots + slot
    misfit[...] = jnp.where(at_slot, jnp.sum(total), 0.0)


def forecast(own, got, direct, passed, near, far, obs_own, obs_got, piece, slot, slots, ncol, total_rows):
    parts = plan(ncol, slot, slots)
    _, worked, kept = parts[piece]
    place = []
    for ct in worked:
        p = 0 if ct in parts[0][0] else 1
        place.append((p, parts[p][0].index(ct)))
    block = jax.ShapeDtypeStruct((3, TILE, len(kept) * LANES), jnp.float32)
    field = pltpu.VMEM((3, len(worked), ROWS, LANES), jnp.float32)
    args = [own, direct, *got, *passed, near, far, obs_own, obs_got]
    return pl.pallas_call(
        functools.partial(
            forecast_kernel,
            worked=worked,
            kept=kept,
            place=place,
            parts=len(got),
            slot=slot,
            slots=slots,
            ncol=ncol,
            total_rows=total_rows,
        ),
        out_shape=[block, block, jax.ShapeDtypeStruct((TILE, LANES), jnp.float32)],
        in_specs=[VMEM] * len(args),
        out_specs=[VMEM] * 3,
        scratch_shapes=[field, field, field, pltpu.VMEM((ROWS, LANES), jnp.float32)],
        compiler_params=pltpu.CompilerParams(vmem_limit_bytes=24 * 2**20),
        cost_estimate=cost(WORK * len(worked)),
    )(*args)


def gather_kernel(*refs, ncol, slots, pieces):
    out = refs[-1]
    par = lax.axis_index("strip") % 2
    for n, (k, p) in enumerate(pieces):
        mine, theirs = refs[2 * n], refs[2 * n + 1]
        for j, ct in enumerate(plan(ncol, k, slots)[p][2]):
            out[par * slots + k, :, :, at(ct)] = mine[:, :, at(j)]
            out[(1 - par) * slots + k, :, :, at(ct)] = theirs[:, :, at(j)]


def gather(blocks, pieces, ncol, slots):
    args = [b for pair in blocks for b in pair]
    return pl.pallas_call(
        functools.partial(gather_kernel, ncol=ncol, slots=slots, pieces=pieces),
        out_shape=jax.ShapeDtypeStruct((2 * slots, 3, TILE, ncol * LANES), jnp.float32),
        in_specs=[VMEM] * len(args),
        out_specs=VMEM,
        compiler_params=pltpu.CompilerParams(vmem_limit_bytes=SMALL),
        cost_estimate=cost(0.1),
    )(*args)


def local(ensemble, offspring, observations, obs_cols, obs_precision):
    members, _, strip_rows, cols = ensemble.shape
    strips = lax.axis_size("strip")
    total_rows = strips * strip_rows
    strip = lax.axis_index("strip")
    half = members // 2
    ncol = cols // LANES

    def moved(even, odd):
        return [(i, (i + (odd if i % 2 else even)) % strips) for i in range(strips)]

    swap = moved(1, -1)
    straight = moved(-2, 2)
    onward = moved(2, -2)
    cross = moved(3, -3)

    arrived = lax.ppermute(ensemble, "particle", [(0, 1), (1, 0)])
    index = sources(offspring, ensemble)

    rows = (strip * strip_rows + jnp.arange(strip_rows, dtype=jnp.int32)).astype(jnp.float32)
    weight = obs_precision * (1.0 + 2.0 * (rows + 0.5) / total_rows)[:, None]
    obs_own = jnp.stack([observations, obs_cols.astype(jnp.float32), weight])

    spans = [
        [(sent[0] * LANES, len(sent) * LANES) for sent, _, _ in plan(ncol, k, half)]
        for k in range(half)
    ]
    kept, given, near, far = pick(index, ensemble, arrived, spans)
    near = lax.ppermute(near, "strip", onward)
    far = lax.ppermute(far, "strip", cross)

    obs_got = lax.ppermute(obs_own, "strip", swap)

    pieces = [(k, p) for k in range(half) for p in range(len(spans[k]))]
    got, passed, direct = [[] for _ in range(half)], [[] for _ in range(half)], []
    swapped, last, blocks, misfits = [], [], [], []
    for n, (k, p) in enumerate(pieces):
        giving, keeping = given[k][p], kept[k]
        if p == 0:
            if k:
                (keeping,) = after((keeping,), last[n - 2])
            direct.append(lax.ppermute(keeping, "strip", straight))
        if n == 1:
            (giving,) = after((giving,), (swapped[0], direct[0], near, far, obs_got))
        elif n == 2:
            (giving,) = after((giving,), (swapped[1], last[0]))
        elif n:
            (giving,) = after((giving,), (swapped[-1], misfits[n - 3]))
        swapped.append(lax.ppermute(giving, "strip", swap))
        goes = swapped[n]
        if n > 1:
            (goes,) = after((goes,), misfits[n - 2])
        last.append(lax.ppermute(goes, "strip", onward))
        got[k].append(swapped[n])
        passed[k].append(last[n])
        keep, send, misfit = forecast(
            kept[k], got[k], direct[k], passed[k], near, far, obs_own, obs_got, p, k, half, ncol, total_rows
        )
        blocks.append((keep, lax.ppermute(send, "strip", swap)))
        misfits.append(misfit)
    total = sum(misfits[1:], misfits[0])
    (total,) = after((total,), [b[1] for b in blocks[:-1]])
    if strips == 8:
        turn = [lax.ppermute(total, "strip", moved(step, step)) for step in (2, 4, 6)]
        total = (total + turn[1]) + (turn[0] + turn[2])
    else:
        step = 2
        while step < strips:
            total = total + lax.ppermute(total, "strip", [(i, i ^ step) for i in range(strips)])
            step *= 2
    theirs = lax.ppermute(total, "strip", swap)
    state = gather(blocks, pieces, ncol, half)
    theirs, total = after((theirs, total), state)
    total = total + theirs
    log_weights = (-0.5 / (total_rows * obs_cols.shape[1])) * total[0, :members]
    return (state, log_weights)


def solution(mesh):
    in_specs = (
        P(("group", "particle"), None, "strip", None),
        P("group"),
        P(("group", "strip"), None),
        P(("group", "strip"), None),
        P(("group", "strip"), None),
    )
    out_specs = (P(("group", "particle"), None, "strip", None), P(("group", "particle")))
    return jax.shard_map(local, mesh=mesh, in_specs=in_specs, out_specs=out_specs, check_vma=False)
```

```python
import functools

import jax
import jax.numpy as jnp
from jax import lax
from jax.experimental import pallas as pl
from jax.experimental.pallas import tpu as pltpu
from jax.sharding import PartitionSpec as P

STEPS = 3
DT = 0.4
HALF = 0.5 * DT
DEPTH = 3 * STEPS
LANES = 128
TILE = 8
BASE = 16
ROWS = 48
SMALL = 12 * 2**20
WORK = 0.005

VMEM = pl.BlockSpec(memory_space=pltpu.VMEM)
SMEM = pl.BlockSpec(memory_space=pltpu.SMEM)
ANY = pl.BlockSpec(memory_space=pl.ANY)


def cost(us):
    return pl.CostEstimate(flops=0, bytes_accessed=int(us * 3.0e6), transcendentals=0)


def plan(ncol, slot, slots):
    every = list(range(ncol))
    if slot < slots - 1:
        return ((every, every, every),)
    cut = ncol // 2 + 2
    return (
        (every[:cut], every[:cut], every[1 : cut - 1]),
        (every[cut:], every[cut - 2 :] + [0, 1], every[cut - 1 :] + [0]),
    )


def after(arrays, first):
    return lax.optimization_barrier((tuple(arrays), first))[0]


def at(i):
    return slice(i * LANES, (i + 1) * LANES)


def index_kernel(offspring, ensemble, index):
    members = index.shape[0]
    here = lax.axis_index("particle")
    cumulative = []
    for i in range(offspring.shape[0]):
        cumulative.append(offspring[i] + (cumulative[-1] if i else 0))
    for k in range(members):
        j = here * members + k
        s = sum((c <= j).astype(jnp.int32) for c in cumulative)
        own = s - here * members
        other = s - (1 - here) * members
        inside = (own >= 0) & (own < members)
        index[k] = jnp.clip(jnp.where(inside, own, members + other), 0, 2 * members - 1)


def sources(offspring, ensemble):
    members = ensemble.shape[0]
    return pl.pallas_call(
        index_kernel,
        out_shape=jax.ShapeDtypeStruct((members,), jnp.int32),
        in_specs=[SMEM, VMEM],
        out_specs=SMEM,
        compiler_params=pltpu.CompilerParams(vmem_limit_bytes=SMALL),
    )(offspring, ensemble)


def pick_kernel(index, own, other, *outs, spans):
    members = own.shape[0]
    half = members // 2
    par = lax.axis_index("strip") % 2
    refs, kept, given = list(outs), [], []
    for s in spans:
        kept.append([refs.pop(0)])
        given.append([refs.pop(0) for _ in s])
    near, far = refs
    wide = own.shape[3] // TILE

    def copy(slot, k, pieces, edge):
        i = index[slot]

        def write(ref, m):
            if len(pieces) == 1:
                pieces[0][...] = ref[m]
            else:
                for (first, count), out in zip(spans[k], pieces):
                    out[...] = ref[m, :, :, pl.ds(first, count)]

            def edges(row):
                for f in range(3):
                    for q in range(TILE):
                        edge[k * 3 + f, q : q + 1, :] = ref[
                            m, f, row : row + 1, q * wide : (q + 1) * wide
                        ]

            @pl.when(par == 0)
            def _():
                edges(TILE - 1)

            @pl.when(par == 1)
            def _():
                edges(0)

        @pl.when(i < members)
        def _():
            write(own, jnp.minimum(i, members - 1))

        @pl.when(i >= members)
        def _():
            write(other, jnp.maximum(i - members, 0))

    for k in range(half):
        copy((1 - par) * half + k, k, given[k], far)
        copy(par * half + k, k, kept[k], near)


def pick(index, own, other, spans):
    shape, kind = own.shape[1:3], own.dtype
    outs = []
    for s in spans:
        outs += [jax.ShapeDtypeStruct(shape + (c,), kind) for c in [own.shape[3]] + [c for _, c in s]]
    outs += [jax.ShapeDtypeStruct((3 * len(spans), TILE, own.shape[3] // TILE), kind)] * 2
    out = pl.pallas_call(
        functools.partial(pick_kernel, spans=spans),
        out_shape=outs,
        in_specs=[SMEM, VMEM, VMEM],
        out_specs=[VMEM] * len(outs),
        compiler_params=pltpu.CompilerParams(vmem_limit_bytes=SMALL),
    )(index, own, other)
    kept, given = [], []
    for s in spans:
        kept.append(out[0])
        given.append(out[1 : 1 + len(s)])
        out = out[1 + len(s) :]
    return kept, given, out[0], out[1]


def evaluate(src, state, dst, cor_ref, start, tiles, kind):
    ncol = src.shape[1]
    lane = lax.broadcasted_iota(jnp.int32, (TILE, LANES), 1)
    first = lane == 0
    last = lane == LANES - 1

    def body(t, carry):
        r0 = start + t * TILE
        rows = pl.ds(r0, TILE)
        cor = cor_ref[rows, :]
        for ct in range(ncol):
            mid, around = [], []
            for f in range(3):
                c = src[f, ct, rows, :]
                e = pltpu.roll(
                    jnp.where(first, src[f, (ct + 1) % ncol, rows, :], c), LANES - 1, 1
                )
                w = pltpu.roll(jnp.where(last, src[f, (ct - 1) % ncol, rows, :], c), 1, 1)
                n = src[f, ct, pl.ds(r0 + 1, TILE), :]
                s = src[f, ct, pl.ds(r0 - 1, TILE), :]
                mid.append(c)
                around.append((e, w, n, s))
            eta, u, v = mid
            (eE, eW, eN, eS), (uE, uW, uN, uS), (vE, vW, vN, vS) = around
            duy = uN - uS
            dvx = vE - vW
            dux = uE - uW
            dvy = vN - vS
            flow = (dux + dvy) + ((eE * uE - eW * uW) + (eN * vN - eS * vS))
            lu = v * (cor - duy) - u * dux - (eE - eW)
            lv = u * (cor + dvx) + v * dvy + (eN - eS)
            change = (-flow, lu, -lv)
            for f in range(3):
                if kind == 0:
                    new = mid[f] + HALF * change[f]
                elif kind == 1:
                    new = 0.75 * state[f, ct, rows, :] + (0.25 * mid[f] + (0.25 * HALF) * change[f])
                else:
                    new = (1.0 / 3.0) * state[f, ct, rows, :] + (
                        (2.0 / 3.0) * mid[f] + (2.0 / 3.0 * HALF) * change[f]
                    )
                dst[f, ct, rows, :] = new
        return carry

    lax.fori_loop(0, tiles, body, 0)


def forecast_kernel(*refs, worked, kept, place, parts, slot, slots, ncol, total_rows):
    own, direct, refs = refs[0], refs[1], refs[2:]
    got, passed = refs[:parts], refs[parts : 2 * parts]
    near, far, obs_own, obs_got, keep, send, misfit, state, s1, s2, cor_ref = refs[2 * parts :]
    strip = lax.axis_index("strip")
    par = strip % 2
    per = ncol // TILE

    def load(own_row, got_row, direct_row, passed_row, near_row, far_row):
        for i, ct in enumerate(worked):
            p, j = place[i]
            for ref, row, place_at in (
                (own, own_row, ct),
                (got[p], got_row, j),
                (direct, direct_row, ct),
                (passed[p], passed_row, j),
            ):
                state[:, i, row : row + TILE, :] = ref[:, :, at(place_at)]
            for ref, row in ((near, near_row), (far, far_row)):
                q = ct // per
                state[:, i, row : row + 1, :] = ref[
                    slot * 3 : slot * 3 + 3, q : q + 1, at(ct % per)
                ]

    above, below = BASE - TILE, BASE + 2 * TILE

    @pl.when(par == 0)
    def _():
        load(BASE, BASE + TILE, below, above, above - 1, below + TILE)

    @pl.when(par == 1)
    def _():
        load(BASE + TILE, BASE, above, below, below + TILE, above - 1)

    row = lax.broadcasted_iota(jnp.int32, (ROWS, LANES), 0) + ((strip - par) * TILE - BASE)
    row = jnp.where(row < 0, row + total_rows, row)
    row = jnp.where(row >= total_rows, row - total_rows, row).astype(jnp.float32)
    cor_ref[...] = 2.0 * (0.3 + 0.4 * ((row + 0.5) / total_rows - 0.5))

    for k in range(DEPTH):
        reach = DEPTH - 1 - k
        tiles = (2 * TILE + 2 * reach + TILE - 1) // TILE
        kind = k % 3
        src, dst = ((state, s1), (s1, s2), (s2, state))[kind]
        evaluate(src, state, dst, cor_ref, BASE - reach, tiles, kind)

    def store(keep_row, send_row):
        for j, ct in enumerate(kept):
            i = worked.index(ct)
            keep[:, :, at(j)] = state[:, i, keep_row : keep_row + TILE, :]
            send[:, :, at(j)] = state[:, i, send_row : send_row + TILE, :]

    @pl.when(par == 0)
    def _():
        store(BASE, BASE + TILE)

    @pl.when(par == 1)
    def _():
        store(BASE + TILE, BASE)

    total = jnp.zeros((TILE, LANES), jnp.float32)
    for side in range(2):
        mine = par == side
        obs = [jnp.where(mine, obs_own[k], obs_got[k]) for k in range(3)]
        where = obs[1].astype(jnp.int32)
        tile, lane = where // LANES, where % LANES
        picked = jnp.zeros((TILE, LANES), jnp.float32)
        here = jnp.zeros((TILE, LANES), jnp.bool_)
        for ct in kept:
            i = worked.index(ct)
            eta = state[0, i, BASE + side * TILE : BASE + (side + 1) * TILE, :]
            found = tile == ct
            picked = jnp.where(found, jnp.take_along_axis(eta, lane, axis=1), picked)
            here = here | found
        gap = obs[0] - picked
        total = total + jnp.where(here, obs[2] * gap * gap, 0.0)
    at_slot = lax.broadcasted_iota(jnp.int32, (TILE, LANES), 1) == par * slots + slot
    misfit[...] = jnp.where(at_slot, jnp.sum(total), 0.0)


def forecast(own, got, direct, passed, near, far, obs_own, obs_got, piece, slot, slots, ncol, total_rows):
    parts = plan(ncol, slot, slots)
    _, worked, kept = parts[piece]
    place = []
    for ct in worked:
        p = 0 if ct in parts[0][0] else 1
        place.append((p, parts[p][0].index(ct)))
    block = jax.ShapeDtypeStruct((3, TILE, len(kept) * LANES), jnp.float32)
    field = pltpu.VMEM((3, len(worked), ROWS, LANES), jnp.float32)
    args = [own, direct, *got, *passed, near, far, obs_own, obs_got]
    return pl.pallas_call(
        functools.partial(
            forecast_kernel,
            worked=worked,
            kept=kept,
            place=place,
            parts=len(got),
            slot=slot,
            slots=slots,
            ncol=ncol,
            total_rows=total_rows,
        ),
        out_shape=[block, block, jax.ShapeDtypeStruct((TILE, LANES), jnp.float32)],
        in_specs=[VMEM] * len(args),
        out_specs=[VMEM] * 3,
        scratch_shapes=[field, field, field, pltpu.VMEM((ROWS, LANES), jnp.float32)],
        compiler_params=pltpu.CompilerParams(vmem_limit_bytes=24 * 2**20),
        cost_estimate=cost(WORK * len(worked)),
    )(*args)


def gather_kernel(*refs, ncol, slots, pieces):
    out = refs[-1]
    par = lax.axis_index("strip") % 2
    for n, (k, p) in enumerate(pieces):
        mine, theirs = refs[2 * n], refs[2 * n + 1]
        for j, ct in enumerate(plan(ncol, k, slots)[p][2]):
            out[par * slots + k, :, :, at(ct)] = mine[:, :, at(j)]
            out[(1 - par) * slots + k, :, :, at(ct)] = theirs[:, :, at(j)]


def gather(blocks, pieces, ncol, slots):
    args = [b for pair in blocks for b in pair]
    return pl.pallas_call(
        functools.partial(gather_kernel, ncol=ncol, slots=slots, pieces=pieces),
        out_shape=jax.ShapeDtypeStruct((2 * slots, 3, TILE, ncol * LANES), jnp.float32),
        in_specs=[VMEM] * len(args),
        out_specs=VMEM,
        compiler_params=pltpu.CompilerParams(vmem_limit_bytes=SMALL),
        cost_estimate=cost(0.1),
    )(*args)


def local(ensemble, offspring, observations, obs_cols, obs_precision):
    members, _, strip_rows, cols = ensemble.shape
    strips = lax.axis_size("strip")
    total_rows = strips * strip_rows
    strip = lax.axis_index("strip")
    half = members // 2
    ncol = cols // LANES

    def moved(even, odd):
        return [(i, (i + (odd if i % 2 else even)) % strips) for i in range(strips)]

    swap = moved(1, -1)
    straight = moved(-2, 2)
    onward = moved(2, -2)
    cross = moved(3, -3)

    arrived = lax.ppermute(ensemble, "particle", [(0, 1), (1, 0)])
    index = sources(offspring, ensemble)

    rows = (strip * strip_rows + jnp.arange(strip_rows, dtype=jnp.int32)).astype(jnp.float32)
    weight = obs_precision * (1.0 + 2.0 * (rows + 0.5) / total_rows)[:, None]
    obs_own = jnp.stack([observations, obs_cols.astype(jnp.float32), weight])

    spans = [
        [(sent[0] * LANES, len(sent) * LANES) for sent, _, _ in plan(ncol, k, half)]
        for k in range(half)
    ]
    kept, given, near, far = pick(index, ensemble, arrived, spans)
    near = lax.ppermute(near, "strip", onward)
    far = lax.ppermute(far, "strip", cross)

    obs_got = lax.ppermute(obs_own, "strip", swap)

    pieces = [(k, p) for k in range(half) for p in range(len(spans[k]))]
    got, passed, direct, blocks, misfits = [], [], [], [], []
    first = None
    for k in range(half):
        giving, keeping = tuple(given[k]), kept[k]
        if k:
            *giving, keeping = after((*giving, keeping), first)
        direct.append(lax.ppermute(keeping, "strip", straight))
        got.append([lax.ppermute(g, "strip", swap) for g in giving])
        passed.append([lax.ppermute(g, "strip", onward) for g in got[k]])
        if first is None:
            first = (direct[0], got[0], near, far, obs_got)
    for k, p in pieces:
        (own,) = after((kept[k],), got[-1])
        keep, send, misfit = forecast(
            own,
            got[k][: p + 1],
            direct[k],
            passed[k][: p + 1],
            near,
            far,
            obs_own,
            obs_got,
            p,
            k,
            half,
            ncol,
            total_rows,
        )
        blocks.append((keep, lax.ppermute(send, "strip", swap)))
        misfits.append(misfit)
    total = sum(misfits[1:], misfits[0])
    (total,) = after((total,), [b[1] for b in blocks[:-1]])
    if strips == 8:
        turn = [lax.ppermute(total, "strip", moved(step, step)) for step in (2, 4, 6)]
        total = (total + turn[1]) + (turn[0] + turn[2])
    else:
        step = 2
        while step < strips:
            total = total + lax.ppermute(total, "strip", [(i, i ^ step) for i in range(strips)])
            step *= 2
    theirs = lax.ppermute(total, "strip", swap)
    state = gather(blocks, pieces, ncol, half)
    theirs, total = after((theirs, total), state)
    total = total + theirs
    log_weights = (-0.5 / (total_rows * obs_cols.shape[1])) * total[0, :members]
    return (state, log_weights)


def solution(mesh):
    in_specs = (
        P(("group", "particle"), None, "strip", None),
        P("group"),
        P(("group", "strip"), None),
        P(("group", "strip"), None),
        P(("group", "strip"), None),
    )
    out_specs = (P(("group", "particle"), None, "strip", None), P(("group", "particle")))
    return jax.shard_map(local, mesh=mesh, in_specs=in_specs, out_specs=out_specs, check_vma=False)
```

```python
import functools

import jax
import jax.numpy as jnp
from jax import lax
from jax.experimental import pallas as pl
from jax.experimental.pallas import tpu as pltpu
from jax.sharding import PartitionSpec as P

STEPS = 3
DT = 0.4
HALF = 0.5 * DT
DEPTH = 3 * STEPS
LANES = 128
TILE = 8
BASE = 16
ROWS = 48
SMALL = 12 * 2**20
WORK = 0.005

VMEM = pl.BlockSpec(memory_space=pltpu.VMEM)
SMEM = pl.BlockSpec(memory_space=pltpu.SMEM)
ANY = pl.BlockSpec(memory_space=pl.ANY)


def cost(us):
    return pl.CostEstimate(flops=0, bytes_accessed=int(us * 3.0e6), transcendentals=0)


def plan(ncol, slot, slots):
    every = list(range(ncol))
    if slot < slots - 1:
        return ((every, every, every),)
    cut = ncol // 2 + 2
    return (
        (every[:cut], every[:cut], every[1 : cut - 1]),
        (every[cut:], every[cut - 2 :] + [0, 1], every[cut - 1 :] + [0]),
    )


def after(arrays, first):
    return lax.optimization_barrier((tuple(arrays), first))[0]


def at(i):
    return slice(i * LANES, (i + 1) * LANES)


def index_kernel(offspring, ensemble, index):
    members = index.shape[0]
    here = lax.axis_index("particle")
    cumulative = []
    for i in range(offspring.shape[0]):
        cumulative.append(offspring[i] + (cumulative[-1] if i else 0))
    for k in range(members):
        j = here * members + k
        s = sum((c <= j).astype(jnp.int32) for c in cumulative)
        own = s - here * members
        other = s - (1 - here) * members
        inside = (own >= 0) & (own < members)
        index[k] = jnp.clip(jnp.where(inside, own, members + other), 0, 2 * members - 1)


def sources(offspring, ensemble):
    members = ensemble.shape[0]
    return pl.pallas_call(
        index_kernel,
        out_shape=jax.ShapeDtypeStruct((members,), jnp.int32),
        in_specs=[SMEM, VMEM],
        out_specs=SMEM,
        compiler_params=pltpu.CompilerParams(vmem_limit_bytes=SMALL),
    )(offspring, ensemble)


def pick_kernel(index, own, other, seen, columns, precision, *outs, spans, total_rows):
    members = own.shape[0]
    half = members // 2
    par = lax.axis_index("strip") % 2
    refs, kept, given = list(outs), [], []
    for s in spans:
        kept.append([refs.pop(0)])
        given.append([refs.pop(0) for _ in s])
    near, far, obs = refs
    cols = own.shape[3]
    wide = cols // TILE
    row = lax.broadcasted_iota(jnp.int32, precision.shape, 0) + lax.axis_index("strip") * TILE
    weight = precision[...] * (1.0 + 2.0 * (row.astype(jnp.float32) + 0.5) / total_rows)
    for n, part in enumerate((seen[...], columns[...].astype(jnp.float32), weight)):
        obs[n] = part
        given[0][0][n, :, cols:] = part

    def copy(slot, k, pieces, edge):
        i = index[slot]

        def write(ref, m):
            if len(pieces) == 1:
                pieces[0][:, :, :cols] = ref[m]
            else:
                for (first, count), out in zip(spans[k], pieces):
                    out[...] = ref[m, :, :, pl.ds(first, count)]

            def edges(row):
                for f in range(3):
                    for q in range(TILE):
                        edge[k * 3 + f, q : q + 1, :] = ref[
                            m, f, row : row + 1, q * wide : (q + 1) * wide
                        ]

            @pl.when(par == 0)
            def _():
                edges(TILE - 1)

            @pl.when(par == 1)
            def _():
                edges(0)

        @pl.when(i < members)
        def _():
            write(own, jnp.minimum(i, members - 1))

        @pl.when(i >= members)
        def _():
            write(other, jnp.maximum(i - members, 0))

    for k in range(half):
        copy((1 - par) * half + k, k, given[k], far)
        copy(par * half + k, k, kept[k], near)


def pick(index, own, other, seen, columns, precision, spans, total_rows):
    shape, kind = own.shape[1:3], own.dtype
    outs = []
    for s in spans:
        widths = [own.shape[3]] + [c for _, c in s]
        if not outs:
            widths[1] += seen.shape[1]
        outs += [jax.ShapeDtypeStruct(shape + (c,), kind) for c in widths]
    outs += [jax.ShapeDtypeStruct((3 * len(spans), TILE, own.shape[3] // TILE), kind)] * 2
    outs.append(jax.ShapeDtypeStruct((3,) + seen.shape, kind))
    out = pl.pallas_call(
        functools.partial(pick_kernel, spans=spans, total_rows=total_rows),
        out_shape=outs,
        in_specs=[SMEM] + [VMEM] * 5,
        out_specs=[VMEM] * len(outs),
        compiler_params=pltpu.CompilerParams(vmem_limit_bytes=SMALL),
    )(index, own, other, seen, columns, precision)
    kept, given = [], []
    for s in spans:
        kept.append(out[0])
        given.append(out[1 : 1 + len(s)])
        out = out[1 + len(s) :]
    return kept, given, out[0], out[1], out[2]


def evaluate(src, state, dst, cor_ref, start, tiles, kind):
    ncol = src.shape[1]
    lane = lax.broadcasted_iota(jnp.int32, (TILE, LANES), 1)
    first = lane == 0
    last = lane == LANES - 1

    def body(t, carry):
        r0 = start + t * TILE
        rows = pl.ds(r0, TILE)
        cor = cor_ref[rows, :]
        for ct in range(ncol):
            mid, around = [], []
            for f in range(3):
                c = src[f, ct, rows, :]
                e = pltpu.roll(
                    jnp.where(first, src[f, (ct + 1) % ncol, rows, :], c), LANES - 1, 1
                )
                w = pltpu.roll(jnp.where(last, src[f, (ct - 1) % ncol, rows, :], c), 1, 1)
                n = src[f, ct, pl.ds(r0 + 1, TILE), :]
                s = src[f, ct, pl.ds(r0 - 1, TILE), :]
                mid.append(c)
                around.append((e, w, n, s))
            eta, u, v = mid
            (eE, eW, eN, eS), (uE, uW, uN, uS), (vE, vW, vN, vS) = around
            duy = uN - uS
            dvx = vE - vW
            dux = uE - uW
            dvy = vN - vS
            flow = (dux + dvy) + ((eE * uE - eW * uW) + (eN * vN - eS * vS))
            lu = v * (cor - duy) - u * dux - (eE - eW)
            lv = u * (cor + dvx) + v * dvy + (eN - eS)
            change = (-flow, lu, -lv)
            for f in range(3):
                if kind == 0:
                    new = mid[f] + HALF * change[f]
                elif kind == 1:
                    new = 0.75 * state[f, ct, rows, :] + (0.25 * mid[f] + (0.25 * HALF) * change[f])
                else:
                    new = (1.0 / 3.0) * state[f, ct, rows, :] + (
                        (2.0 / 3.0) * mid[f] + (2.0 / 3.0 * HALF) * change[f]
                    )
                dst[f, ct, rows, :] = new
        return carry

    lax.fori_loop(0, tiles, body, 0)


def forecast_kernel(*refs, worked, kept, place, parts, slot, slots, ncol, total_rows):
    own, direct, refs = refs[0], refs[1], refs[2:]
    got, passed = refs[:parts], refs[parts : 2 * parts]
    near, far, obs_own, obs_got, keep, send, misfit, state, s1, s2, cor_ref = refs[2 * parts :]
    behind = obs_got.shape[2] - LANES
    strip = lax.axis_index("strip")
    par = strip % 2
    per = ncol // TILE

    def load(own_row, got_row, direct_row, passed_row, near_row, far_row):
        for i, ct in enumerate(worked):
            p, j = place[i]
            for ref, row, place_at in (
                (own, own_row, ct),
                (got[p], got_row, j),
                (direct, direct_row, ct),
                (passed[p], passed_row, j),
            ):
                state[:, i, row : row + TILE, :] = ref[:, :, at(place_at)]
            for ref, row in ((near, near_row), (far, far_row)):
                q = ct // per
                state[:, i, row : row + 1, :] = ref[
                    slot * 3 : slot * 3 + 3, q : q + 1, at(ct % per)
                ]

    above, below = BASE - TILE, BASE + 2 * TILE

    @pl.when(par == 0)
    def _():
        load(BASE, BASE + TILE, below, above, above - 1, below + TILE)

    @pl.when(par == 1)
    def _():
        load(BASE + TILE, BASE, above, below, below + TILE, above - 1)

    row = lax.broadcasted_iota(jnp.int32, (ROWS, LANES), 0) + ((strip - par) * TILE - BASE)
    row = jnp.where(row < 0, row + total_rows, row)
    row = jnp.where(row >= total_rows, row - total_rows, row).astype(jnp.float32)
    cor_ref[...] = 2.0 * (0.3 + 0.4 * ((row + 0.5) / total_rows - 0.5))

    for k in range(DEPTH):
        reach = DEPTH - 1 - k
        tiles = (2 * TILE + 2 * reach + TILE - 1) // TILE
        kind = k % 3
        src, dst = ((state, s1), (s1, s2), (s2, state))[kind]
        evaluate(src, state, dst, cor_ref, BASE - reach, tiles, kind)

    def store(keep_row, send_row):
        for j, ct in enumerate(kept):
            i = worked.index(ct)
            keep[:, :, at(j)] = state[:, i, keep_row : keep_row + TILE, :]
            send[:, :, at(j)] = state[:, i, send_row : send_row + TILE, :]

    @pl.when(par == 0)
    def _():
        store(BASE, BASE + TILE)

    @pl.when(par == 1)
    def _():
        store(BASE + TILE, BASE)

    total = jnp.zeros((TILE, LANES), jnp.float32)
    for side in range(2):
        mine = par == side
        obs = [jnp.where(mine, obs_own[k], obs_got[k, :, behind:]) for k in range(3)]
        where = obs[1].astype(jnp.int32)
        tile, lane = where // LANES, where % LANES
        picked = jnp.zeros((TILE, LANES), jnp.float32)
        here = jnp.zeros((TILE, LANES), jnp.bool_)
        for ct in kept:
            i = worked.index(ct)
            eta = state[0, i, BASE + side * TILE : BASE + (side + 1) * TILE, :]
            found = tile == ct
            picked = jnp.where(found, jnp.take_along_axis(eta, lane, axis=1), picked)
            here = here | found
        gap = obs[0] - picked
        total = total + jnp.where(here, obs[2] * gap * gap, 0.0)
    at_slot = lax.broadcasted_iota(jnp.int32, (TILE, LANES), 1) == par * slots + slot
    misfit[...] = jnp.where(at_slot, jnp.sum(total), 0.0)


def forecast(own, got, direct, passed, near, far, obs_own, obs_got, piece, slot, slots, ncol, total_rows):
    parts = plan(ncol, slot, slots)
    _, worked, kept = parts[piece]
    place = []
    for ct in worked:
        p = 0 if ct in parts[0][0] else 1
        place.append((p, parts[p][0].index(ct)))
    block = jax.ShapeDtypeStruct((3, TILE, len(kept) * LANES), jnp.float32)
    field = pltpu.VMEM((3, len(worked), ROWS, LANES), jnp.float32)
    args = [own, direct, *got, *passed, near, far, obs_own, obs_got]
    return pl.pallas_call(
        functools.partial(
            forecast_kernel,
            worked=worked,
            kept=kept,
            place=place,
            parts=len(got),
            slot=slot,
            slots=slots,
            ncol=ncol,
            total_rows=total_rows,
        ),
        out_shape=[block, block, jax.ShapeDtypeStruct((TILE, LANES), jnp.float32)],
        in_specs=[VMEM] * len(args),
        out_specs=[VMEM] * 3,
        scratch_shapes=[field, field, field, pltpu.VMEM((ROWS, LANES), jnp.float32)],
        compiler_params=pltpu.CompilerParams(vmem_limit_bytes=24 * 2**20),
        cost_estimate=cost(WORK * len(worked)),
    )(*args)


def gather_kernel(*refs, ncol, slots, pieces):
    out = refs[-1]
    par = lax.axis_index("strip") % 2
    for n, (k, p) in enumerate(pieces):
        mine, theirs = refs[2 * n], refs[2 * n + 1]
        for j, ct in enumerate(plan(ncol, k, slots)[p][2]):
            out[par * slots + k, :, :, at(ct)] = mine[:, :, at(j)]
            out[(1 - par) * slots + k, :, :, at(ct)] = theirs[:, :, at(j)]


def gather(blocks, pieces, ncol, slots):
    args = [b for pair in blocks for b in pair]
    return pl.pallas_call(
        functools.partial(gather_kernel, ncol=ncol, slots=slots, pieces=pieces),
        out_shape=jax.ShapeDtypeStruct((2 * slots, 3, TILE, ncol * LANES), jnp.float32),
        in_specs=[VMEM] * len(args),
        out_specs=VMEM,
        compiler_params=pltpu.CompilerParams(vmem_limit_bytes=SMALL),
        cost_estimate=cost(0.1),
    )(*args)


def local(ensemble, offspring, observations, obs_cols, obs_precision):
    members, _, strip_rows, cols = ensemble.shape
    strips = lax.axis_size("strip")
    total_rows = strips * strip_rows
    strip = lax.axis_index("strip")
    half = members // 2
    ncol = cols // LANES

    def moved(even, odd):
        return [(i, (i + (odd if i % 2 else even)) % strips) for i in range(strips)]

    swap = moved(1, -1)
    straight = moved(-2, 2)
    onward = moved(2, -2)
    cross = moved(3, -3)

    arrived = lax.ppermute(ensemble, "particle", [(0, 1), (1, 0)])
    index = sources(offspring, ensemble)

    spans = [
        [(sent[0] * LANES, len(sent) * LANES) for sent, _, _ in plan(ncol, k, half)]
        for k in range(half)
    ]
    kept, given, near, far, obs_own = pick(
        index, ensemble, arrived, observations, obs_cols, obs_precision, spans, total_rows
    )
    near = lax.ppermute(near, "strip", onward)
    far = lax.ppermute(far, "strip", cross)


    pieces = [(k, p) for k in range(half) for p in range(len(spans[k]))]
    got, passed, direct, blocks, misfits = [], [], [], [], []
    for k in range(half):
        giving, keeping = tuple(given[k]), kept[k]
        if k:
            giving = after(giving, got[0])
            (keeping,) = after((keeping,), (direct[0], got[0], near, far))
        direct.append(lax.ppermute(keeping, "strip", straight))
        got.append([lax.ppermute(g, "strip", swap) for g in giving])
        passed.append([lax.ppermute(g, "strip", onward) for g in got[k]])
    obs_got = got[0][0]
    for k, p in pieces:
        (own,) = after((kept[k],), got[-1])
        keep, send, misfit = forecast(
            own,
            got[k][: p + 1],
            direct[k],
            passed[k][: p + 1],
            near,
            far,
            obs_own,
            obs_got,
            p,
            k,
            half,
            ncol,
            total_rows,
        )
        blocks.append((keep, lax.ppermute(send, "strip", swap)))
        misfits.append(misfit)
    total = sum(misfits[1:], misfits[0])
    (total,) = after((total,), [b[1] for b in blocks[:-1]])
    if strips == 8:
        turn = [lax.ppermute(total, "strip", moved(step, step)) for step in (2, 4, 6)]
        total = (total + turn[1]) + (turn[0] + turn[2])
    else:
        step = 2
        while step < strips:
            total = total + lax.ppermute(total, "strip", [(i, i ^ step) for i in range(strips)])
            step *= 2
    (total,) = after((total,), blocks[-1][1])
    theirs = lax.ppermute(total, "strip", swap)
    state = gather(blocks, pieces, ncol, half)
    theirs, total = after((theirs, total), state)
    total = total + theirs
    log_weights = (-0.5 / (total_rows * obs_cols.shape[1])) * total[0, :members]
    return (state, log_weights)


def solution(mesh):
    in_specs = (
        P(("group", "particle"), None, "strip", None),
        P("group"),
        P(("group", "strip"), None),
        P(("group", "strip"), None),
        P(("group", "strip"), None),
    )
    out_specs = (P(("group", "particle"), None, "strip", None), P(("group", "particle")))
    return jax.shard_map(local, mesh=mesh, in_specs=in_specs, out_specs=out_specs, check_vma=False)
```

```python
import functools

import jax
import jax.numpy as jnp
from jax import lax
from jax.experimental import pallas as pl
from jax.experimental.pallas import tpu as pltpu
from jax.sharding import PartitionSpec as P

STEPS = 3
DT = 0.4
HALF = 0.5 * DT
DEPTH = 3 * STEPS
LANES = 128
TILE = 8
BASE = 16
ROWS = 48
SMALL = 12 * 2**20
WORK = 0.005

VMEM = pl.BlockSpec(memory_space=pltpu.VMEM)
SMEM = pl.BlockSpec(memory_space=pltpu.SMEM)
ANY = pl.BlockSpec(memory_space=pl.ANY)


def cost(us):
    return pl.CostEstimate(flops=0, bytes_accessed=int(us * 3.0e6), transcendentals=0)


def plan(ncol, slot, slots):
    every = list(range(ncol))
    if slot < slots - 1:
        return ((every, every, every),)
    cut = ncol // 2 + 2
    return (
        (every[:cut], every[:cut], every[1 : cut - 1]),
        (every[cut:], every[cut - 2 :] + [0, 1], every[cut - 1 :] + [0]),
    )


def after(arrays, first):
    return lax.optimization_barrier((tuple(arrays), first))[0]


def at(i):
    return slice(i * LANES, (i + 1) * LANES)


def index_kernel(offspring, ensemble, index):
    members = index.shape[0]
    here = lax.axis_index("particle")
    cumulative = []
    for i in range(offspring.shape[0]):
        cumulative.append(offspring[i] + (cumulative[-1] if i else 0))
    for k in range(members):
        j = here * members + k
        s = sum((c <= j).astype(jnp.int32) for c in cumulative)
        own = s - here * members
        other = s - (1 - here) * members
        inside = (own >= 0) & (own < members)
        index[k] = jnp.clip(jnp.where(inside, own, members + other), 0, 2 * members - 1)


def sources(offspring, ensemble):
    members = ensemble.shape[0]
    return pl.pallas_call(
        index_kernel,
        out_shape=jax.ShapeDtypeStruct((members,), jnp.int32),
        in_specs=[SMEM, VMEM],
        out_specs=SMEM,
        compiler_params=pltpu.CompilerParams(vmem_limit_bytes=SMALL),
    )(offspring, ensemble)


def pick_kernel(index, own, other, *outs, spans):
    members = own.shape[0]
    half = members // 2
    par = lax.axis_index("strip") % 2
    refs, kept, given = list(outs), [], []
    for s in spans:
        kept.append([refs.pop(0)])
        given.append([refs.pop(0) for _ in s])
    near, far = refs
    wide = own.shape[3] // TILE

    def copy(slot, k, pieces, edge):
        i = index[slot]

        def write(ref, m):
            if len(pieces) == 1:
                pieces[0][...] = ref[m]
            else:
                for (first, count), out in zip(spans[k], pieces):
                    out[...] = ref[m, :, :, pl.ds(first, count)]

            def edges(row):
                for f in range(3):
                    for q in range(TILE):
                        edge[k * 3 + f, q : q + 1, :] = ref[
                            m, f, row : row + 1, q * wide : (q + 1) * wide
                        ]

            @pl.when(par == 0)
            def _():
                edges(TILE - 1)

            @pl.when(par == 1)
            def _():
                edges(0)

        @pl.when(i < members)
        def _():
            write(own, jnp.minimum(i, members - 1))

        @pl.when(i >= members)
        def _():
            write(other, jnp.maximum(i - members, 0))

    for k in range(half):
        copy((1 - par) * half + k, k, given[k], far)
        copy(par * half + k, k, kept[k], near)


def pick(index, own, other, spans):
    shape, kind = own.shape[1:3], own.dtype
    outs = []
    for s in spans:
        outs += [jax.ShapeDtypeStruct(shape + (c,), kind) for c in [own.shape[3]] + [c for _, c in s]]
    outs += [jax.ShapeDtypeStruct((3 * len(spans), TILE, own.shape[3] // TILE), kind)] * 2
    out = pl.pallas_call(
        functools.partial(pick_kernel, spans=spans),
        out_shape=outs,
        in_specs=[SMEM, VMEM, VMEM],
        out_specs=[VMEM] * len(outs),
        compiler_params=pltpu.CompilerParams(vmem_limit_bytes=SMALL),
    )(index, own, other)
    kept, given = [], []
    for s in spans:
        kept.append(out[0])
        given.append(out[1 : 1 + len(s)])
        out = out[1 + len(s) :]
    return kept, given, out[0], out[1]


def evaluate(src, state, dst, cor_ref, start, tiles, kind):
    ncol = src.shape[1]
    lane = lax.broadcasted_iota(jnp.int32, (TILE, LANES), 1)
    first = lane == 0
    last = lane == LANES - 1

    def body(t, carry):
        r0 = start + t * TILE
        rows = pl.ds(r0, TILE)
        cor = cor_ref[rows, :]
        for ct in range(ncol):
            mid, around = [], []
            for f in range(3):
                c = src[f, ct, rows, :]
                e = pltpu.roll(
                    jnp.where(first, src[f, (ct + 1) % ncol, rows, :], c), LANES - 1, 1
                )
                w = pltpu.roll(jnp.where(last, src[f, (ct - 1) % ncol, rows, :], c), 1, 1)
                n = src[f, ct, pl.ds(r0 + 1, TILE), :]
                s = src[f, ct, pl.ds(r0 - 1, TILE), :]
                mid.append(c)
                around.append((e, w, n, s))
            eta, u, v = mid
            (eE, eW, eN, eS), (uE, uW, uN, uS), (vE, vW, vN, vS) = around
            duy = uN - uS
            dvx = vE - vW
            dux = uE - uW
            dvy = vN - vS
            flow = (dux + dvy) + ((eE * uE - eW * uW) + (eN * vN - eS * vS))
            lu = v * (cor - duy) - u * dux - (eE - eW)
            lv = u * (cor + dvx) + v * dvy + (eN - eS)
            change = (-flow, lu, -lv)
            for f in range(3):
                if kind == 0:
                    new = mid[f] + HALF * change[f]
                elif kind == 1:
                    new = 0.75 * state[f, ct, rows, :] + (0.25 * mid[f] + (0.25 * HALF) * change[f])
                else:
                    new = (1.0 / 3.0) * state[f, ct, rows, :] + (
                        (2.0 / 3.0) * mid[f] + (2.0 / 3.0 * HALF) * change[f]
                    )
                dst[f, ct, rows, :] = new
        return carry

    lax.fori_loop(0, tiles, body, 0)


def forecast_kernel(*refs, worked, kept, place, parts, slot, slots, ncol, total_rows):
    own, direct, refs = refs[0], refs[1], refs[2:]
    got, passed = refs[:parts], refs[parts : 2 * parts]
    near, far, obs_own, obs_got, keep, send, misfit, state, s1, s2, cor_ref = refs[2 * parts :]
    strip = lax.axis_index("strip")
    par = strip % 2
    per = ncol // TILE

    def load(own_row, got_row, direct_row, passed_row, near_row, far_row):
        for i, ct in enumerate(worked):
            p, j = place[i]
            for ref, row, place_at in (
                (own, own_row, ct),
                (got[p], got_row, j),
                (direct, direct_row, ct),
                (passed[p], passed_row, j),
            ):
                state[:, i, row : row + TILE, :] = ref[:, :, at(place_at)]
            for ref, row in ((near, near_row), (far, far_row)):
                q = ct // per
                state[:, i, row : row + 1, :] = ref[
                    slot * 3 : slot * 3 + 3, q : q + 1, at(ct % per)
                ]

    above, below = BASE - TILE, BASE + 2 * TILE

    @pl.when(par == 0)
    def _():
        load(BASE, BASE + TILE, below, above, above - 1, below + TILE)

    @pl.when(par == 1)
    def _():
        load(BASE + TILE, BASE, above, below, below + TILE, above - 1)

    row = lax.broadcasted_iota(jnp.int32, (ROWS, LANES), 0) + ((strip - par) * TILE - BASE)
    row = jnp.where(row < 0, row + total_rows, row)
    row = jnp.where(row >= total_rows, row - total_rows, row).astype(jnp.float32)
    cor_ref[...] = 2.0 * (0.3 + 0.4 * ((row + 0.5) / total_rows - 0.5))

    for k in range(DEPTH):
        reach = DEPTH - 1 - k
        tiles = (2 * TILE + 2 * reach + TILE - 1) // TILE
        kind = k % 3
        src, dst = ((state, s1), (s1, s2), (s2, state))[kind]
        evaluate(src, state, dst, cor_ref, BASE - reach, tiles, kind)

    def store(keep_row, send_row):
        for j, ct in enumerate(kept):
            i = worked.index(ct)
            keep[:, :, at(j)] = state[:, i, keep_row : keep_row + TILE, :]
            send[:, :, at(j)] = state[:, i, send_row : send_row + TILE, :]

    @pl.when(par == 0)
    def _():
        store(BASE, BASE + TILE)

    @pl.when(par == 1)
    def _():
        store(BASE + TILE, BASE)

    total = jnp.zeros((TILE, LANES), jnp.float32)
    for side in range(2):
        mine = par == side
        obs = [jnp.where(mine, obs_own[k], obs_got[k]) for k in range(3)]
        where = obs[1].astype(jnp.int32)
        tile, lane = where // LANES, where % LANES
        picked = jnp.zeros((TILE, LANES), jnp.float32)
        here = jnp.zeros((TILE, LANES), jnp.bool_)
        for ct in kept:
            i = worked.index(ct)
            eta = state[0, i, BASE + side * TILE : BASE + (side + 1) * TILE, :]
            found = tile == ct
            picked = jnp.where(found, jnp.take_along_axis(eta, lane, axis=1), picked)
            here = here | found
        gap = obs[0] - picked
        total = total + jnp.where(here, obs[2] * gap * gap, 0.0)
    at_slot = lax.broadcasted_iota(jnp.int32, (TILE, LANES), 1) == par * slots + slot
    misfit[...] = jnp.where(at_slot, jnp.sum(total), 0.0)


def forecast(own, got, direct, passed, near, far, obs_own, obs_got, piece, slot, slots, ncol, total_rows):
    parts = plan(ncol, slot, slots)
    _, worked, kept = parts[piece]
    place = []
    for ct in worked:
        p = 0 if ct in parts[0][0] else 1
        place.append((p, parts[p][0].index(ct)))
    block = jax.ShapeDtypeStruct((3, TILE, len(kept) * LANES), jnp.float32)
    field = pltpu.VMEM((3, len(worked), ROWS, LANES), jnp.float32)
    args = [own, direct, *got, *passed, near, far, obs_own, obs_got]
    return pl.pallas_call(
        functools.partial(
            forecast_kernel,
            worked=worked,
            kept=kept,
            place=place,
            parts=len(got),
            slot=slot,
            slots=slots,
            ncol=ncol,
            total_rows=total_rows,
        ),
        out_shape=[block, block, jax.ShapeDtypeStruct((TILE, LANES), jnp.float32)],
        in_specs=[VMEM] * len(args),
        out_specs=[VMEM] * 3,
        scratch_shapes=[field, field, field, pltpu.VMEM((ROWS, LANES), jnp.float32)],
        compiler_params=pltpu.CompilerParams(vmem_limit_bytes=24 * 2**20),
        cost_estimate=cost(WORK * len(worked)),
    )(*args)


def gather_kernel(*refs, ncol, slots, pieces):
    out = refs[-1]
    par = lax.axis_index("strip") % 2
    for n, (k, p) in enumerate(pieces):
        mine, theirs = refs[2 * n], refs[2 * n + 1]
        for j, ct in enumerate(plan(ncol, k, slots)[p][2]):
            out[par * slots + k, :, :, at(ct)] = mine[:, :, at(j)]
            out[(1 - par) * slots + k, :, :, at(ct)] = theirs[:, :, at(j)]


def gather(blocks, pieces, ncol, slots):
    args = [b for pair in blocks for b in pair]
    return pl.pallas_call(
        functools.partial(gather_kernel, ncol=ncol, slots=slots, pieces=pieces),
        out_shape=jax.ShapeDtypeStruct((2 * slots, 3, TILE, ncol * LANES), jnp.float32),
        in_specs=[VMEM] * len(args),
        out_specs=VMEM,
        compiler_params=pltpu.CompilerParams(vmem_limit_bytes=SMALL),
        cost_estimate=cost(0.1),
    )(*args)


def local(ensemble, offspring, observations, obs_cols, obs_precision):
    members, _, strip_rows, cols = ensemble.shape
    strips = lax.axis_size("strip")
    total_rows = strips * strip_rows
    strip = lax.axis_index("strip")
    half = members // 2
    ncol = cols // LANES

    def moved(even, odd):
        return [(i, (i + (odd if i % 2 else even)) % strips) for i in range(strips)]

    swap = moved(1, -1)
    straight = moved(-2, 2)
    onward = moved(2, -2)
    cross = moved(3, -3)

    arrived = lax.ppermute(ensemble, "particle", [(0, 1), (1, 0)])
    index = sources(offspring, ensemble)

    rows = (strip * strip_rows + jnp.arange(strip_rows, dtype=jnp.int32)).astype(jnp.float32)
    weight = obs_precision * (1.0 + 2.0 * (rows + 0.5) / total_rows)[:, None]
    obs_own = jnp.stack([observations, obs_cols.astype(jnp.float32), weight])

    spans = [
        [(sent[0] * LANES, len(sent) * LANES) for sent, _, _ in plan(ncol, k, half)]
        for k in range(half)
    ]
    kept, given, near, far = pick(index, ensemble, arrived, spans)
    near = lax.ppermute(near, "strip", onward)
    far = lax.ppermute(far, "strip", cross)

    obs_got = lax.ppermute(obs_own, "strip", swap)

    pieces = [(k, p) for k in range(half) for p in range(len(spans[k]))]
    got, passed, direct, blocks, misfits = [], [], [], [], []
    first = None
    for k in range(half):
        giving, keeping = tuple(given[k]), kept[k]
        if k:
            giving = after(giving, first)
        got.append([lax.ppermute(g, "strip", swap) for g in giving])
        if k:
            (keeping,) = after((keeping,), (got[k][0], obs_got))
        direct.append(lax.ppermute(keeping, "strip", straight))
        passed.append([lax.ppermute(g, "strip", onward) for g in got[k]])
        if first is None:
            first = (got[0], near, far)
    for k, p in pieces:
        (own,) = after((kept[k],), (got[-1], misfits[-1:]))
        keep, send, misfit = forecast(
            own,
            got[k][: p + 1],
            direct[k],
            passed[k][: p + 1],
            near,
            far,
            obs_own,
            obs_got,
            p,
            k,
            half,
            ncol,
            total_rows,
        )
        blocks.append((keep, lax.ppermute(send, "strip", swap)))
        misfits.append(misfit)
    total = sum(misfits[1:], misfits[0])
    (total,) = after((total,), [b[1] for b in blocks[:-1]])
    if strips == 8:
        turn = [lax.ppermute(total, "strip", moved(step, step)) for step in (2, 4, 6)]
        total = (total + turn[1]) + (turn[0] + turn[2])
    else:
        step = 2
        while step < strips:
            total = total + lax.ppermute(total, "strip", [(i, i ^ step) for i in range(strips)])
            step *= 2
    theirs = lax.ppermute(total, "strip", swap)
    state = gather(blocks, pieces, ncol, half)
    theirs, total = after((theirs, total), state)
    total = total + theirs
    log_weights = (-0.5 / (total_rows * obs_cols.shape[1])) * total[0, :members]
    return (state, log_weights)


def solution(mesh):
    in_specs = (
        P(("group", "particle"), None, "strip", None),
        P("group"),
        P(("group", "strip"), None),
        P(("group", "strip"), None),
        P(("group", "strip"), None),
    )
    out_specs = (P(("group", "particle"), None, "strip", None), P(("group", "particle")))
    return jax.shard_map(local, mesh=mesh, in_specs=in_specs, out_specs=out_specs, check_vma=False)
```

```python
import functools

import jax
import jax.numpy as jnp
from jax import lax
from jax.experimental import pallas as pl
from jax.experimental.pallas import tpu as pltpu
from jax.sharding import PartitionSpec as P

STEPS = 3
DT = 0.4
HALF = 0.5 * DT
DEPTH = 3 * STEPS
LANES = 128
TILE = 8
BASE = 16
ROWS = 48
SMALL = 12 * 2**20
WORK = 0.005

VMEM = pl.BlockSpec(memory_space=pltpu.VMEM)
SMEM = pl.BlockSpec(memory_space=pltpu.SMEM)
ANY = pl.BlockSpec(memory_space=pl.ANY)


def cost(us):
    return pl.CostEstimate(flops=0, bytes_accessed=int(us * 3.0e6), transcendentals=0)


def plan(ncol, slot, slots):
    every = list(range(ncol))
    if slot < slots - 1:
        return ((every, every, every),)
    cut = ncol // 2 + 2
    return (
        (every[:cut], every[:cut], every[1 : cut - 1]),
        (every[cut:], every[cut - 2 :] + [0, 1], every[cut - 1 :] + [0]),
    )


def after(arrays, first):
    return lax.optimization_barrier((tuple(arrays), first))[0]


def at(i):
    return slice(i * LANES, (i + 1) * LANES)


def index_kernel(offspring, ensemble, index):
    members = index.shape[0]
    here = lax.axis_index("particle")
    cumulative = []
    for i in range(offspring.shape[0]):
        cumulative.append(offspring[i] + (cumulative[-1] if i else 0))
    for k in range(members):
        j = here * members + k
        s = sum((c <= j).astype(jnp.int32) for c in cumulative)
        own = s - here * members
        other = s - (1 - here) * members
        inside = (own >= 0) & (own < members)
        index[k] = jnp.clip(jnp.where(inside, own, members + other), 0, 2 * members - 1)


def sources(offspring, ensemble):
    members = ensemble.shape[0]
    return pl.pallas_call(
        index_kernel,
        out_shape=jax.ShapeDtypeStruct((members,), jnp.int32),
        in_specs=[SMEM, VMEM],
        out_specs=SMEM,
        compiler_params=pltpu.CompilerParams(vmem_limit_bytes=SMALL),
    )(offspring, ensemble)


def pick_kernel(index, own, other, *outs, spans):
    members = own.shape[0]
    half = members // 2
    par = lax.axis_index("strip") % 2
    refs, kept, given = list(outs), [], []
    for s in spans:
        kept.append([refs.pop(0)])
        given.append([refs.pop(0) for _ in s])
    near, far = refs
    wide = own.shape[3] // TILE

    def copy(slot, k, pieces, edge):
        i = index[slot]

        def write(ref, m):
            if len(pieces) == 1:
                pieces[0][...] = ref[m]
            else:
                for (first, count), out in zip(spans[k], pieces):
                    out[...] = ref[m, :, :, pl.ds(first, count)]

            def edges(row):
                for f in range(3):
                    for q in range(TILE):
                        edge[k * 3 + f, q : q + 1, :] = ref[
                            m, f, row : row + 1, q * wide : (q + 1) * wide
                        ]

            @pl.when(par == 0)
            def _():
                edges(TILE - 1)

            @pl.when(par == 1)
            def _():
                edges(0)

        @pl.when(i < members)
        def _():
            write(own, jnp.minimum(i, members - 1))

        @pl.when(i >= members)
        def _():
            write(other, jnp.maximum(i - members, 0))

    for k in range(half):
        copy((1 - par) * half + k, k, given[k], far)
        copy(par * half + k, k, kept[k], near)


def pick(index, own, other, spans):
    shape, kind = own.shape[1:3], own.dtype
    outs = []
    for s in spans:
        outs += [jax.ShapeDtypeStruct(shape + (c,), kind) for c in [own.shape[3]] + [c for _, c in s]]
    outs += [jax.ShapeDtypeStruct((3 * len(spans), TILE, own.shape[3] // TILE), kind)] * 2
    out = pl.pallas_call(
        functools.partial(pick_kernel, spans=spans),
        out_shape=outs,
        in_specs=[SMEM, VMEM, VMEM],
        out_specs=[VMEM] * len(outs),
        compiler_params=pltpu.CompilerParams(vmem_limit_bytes=SMALL),
    )(index, own, other)
    kept, given = [], []
    for s in spans:
        kept.append(out[0])
        given.append(out[1 : 1 + len(s)])
        out = out[1 + len(s) :]
    return kept, given, out[0], out[1]


def evaluate(src, state, dst, cor_ref, start, tiles, kind):
    ncol = src.shape[1]
    lane = lax.broadcasted_iota(jnp.int32, (TILE, LANES), 1)
    first = lane == 0
    last = lane == LANES - 1

    def body(t, carry):
        r0 = start + t * TILE
        rows = pl.ds(r0, TILE)
        cor = cor_ref[rows, :]
        for ct in range(ncol):
            mid, around = [], []
            for f in range(3):
                c = src[f, ct, rows, :]
                e = pltpu.roll(
                    jnp.where(first, src[f, (ct + 1) % ncol, rows, :], c), LANES - 1, 1
                )
                w = pltpu.roll(jnp.where(last, src[f, (ct - 1) % ncol, rows, :], c), 1, 1)
                n = src[f, ct, pl.ds(r0 + 1, TILE), :]
                s = src[f, ct, pl.ds(r0 - 1, TILE), :]
                mid.append(c)
                around.append((e, w, n, s))
            eta, u, v = mid
            (eE, eW, eN, eS), (uE, uW, uN, uS), (vE, vW, vN, vS) = around
            duy = uN - uS
            dvx = vE - vW
            dux = uE - uW
            dvy = vN - vS
            flow = (dux + dvy) + ((eE * uE - eW * uW) + (eN * vN - eS * vS))
            lu = v * (cor - duy) - u * dux - (eE - eW)
            lv = u * (cor + dvx) + v * dvy + (eN - eS)
            change = (-flow, lu, -lv)
            for f in range(3):
                if kind == 0:
                    new = mid[f] + HALF * change[f]
                elif kind == 1:
                    new = 0.75 * state[f, ct, rows, :] + (0.25 * mid[f] + (0.25 * HALF) * change[f])
                else:
                    new = (1.0 / 3.0) * state[f, ct, rows, :] + (
                        (2.0 / 3.0) * mid[f] + (2.0 / 3.0 * HALF) * change[f]
                    )
                dst[f, ct, rows, :] = new
        return carry

    lax.fori_loop(0, tiles, body, 0)


def forecast_kernel(*refs, worked, kept, place, parts, slot, slots, ncol, total_rows):
    own, direct, refs = refs[0], refs[1], refs[2:]
    got, passed = refs[:parts], refs[parts : 2 * parts]
    near, far, obs_own, obs_got, keep, send, misfit, state, s1, s2, cor_ref = refs[2 * parts :]
    strip = lax.axis_index("strip")
    par = strip % 2
    per = ncol // TILE

    def load(own_row, got_row, direct_row, passed_row, near_row, far_row):
        for i, ct in enumerate(worked):
            p, j = place[i]
            for ref, row, place_at in (
                (own, own_row, ct),
                (got[p], got_row, j),
                (direct, direct_row, ct),
                (passed[p], passed_row, j),
            ):
                state[:, i, row : row + TILE, :] = ref[:, :, at(place_at)]
            for ref, row in ((near, near_row), (far, far_row)):
                q = ct // per
                state[:, i, row : row + 1, :] = ref[
                    slot * 3 : slot * 3 + 3, q : q + 1, at(ct % per)
                ]

    above, below = BASE - TILE, BASE + 2 * TILE

    @pl.when(par == 0)
    def _():
        load(BASE, BASE + TILE, below, above, above - 1, below + TILE)

    @pl.when(par == 1)
    def _():
        load(BASE + TILE, BASE, above, below, below + TILE, above - 1)

    row = lax.broadcasted_iota(jnp.int32, (ROWS, LANES), 0) + ((strip - par) * TILE - BASE)
    row = jnp.where(row < 0, row + total_rows, row)
    row = jnp.where(row >= total_rows, row - total_rows, row).astype(jnp.float32)
    cor_ref[...] = 2.0 * (0.3 + 0.4 * ((row + 0.5) / total_rows - 0.5))

    for k in range(DEPTH):
        reach = DEPTH - 1 - k
        tiles = (2 * TILE + 2 * reach + TILE - 1) // TILE
        kind = k % 3
        src, dst = ((state, s1), (s1, s2), (s2, state))[kind]
        evaluate(src, state, dst, cor_ref, BASE - reach, tiles, kind)

    def store(keep_row, send_row):
        for j, ct in enumerate(kept):
            i = worked.index(ct)
            keep[:, :, at(j)] = state[:, i, keep_row : keep_row + TILE, :]
            send[:, :, at(j)] = state[:, i, send_row : send_row + TILE, :]

    @pl.when(par == 0)
    def _():
        store(BASE, BASE + TILE)

    @pl.when(par == 1)
    def _():
        store(BASE + TILE, BASE)

    total = jnp.zeros((TILE, LANES), jnp.float32)
    for side in range(2):
        mine = par == side
        obs = [jnp.where(mine, obs_own[k], obs_got[k]) for k in range(3)]
        where = obs[1].astype(jnp.int32)
        tile, lane = where // LANES, where % LANES
        picked = jnp.zeros((TILE, LANES), jnp.float32)
        here = jnp.zeros((TILE, LANES), jnp.bool_)
        for ct in kept:
            i = worked.index(ct)
            eta = state[0, i, BASE + side * TILE : BASE + (side + 1) * TILE, :]
            found = tile == ct
            picked = jnp.where(found, jnp.take_along_axis(eta, lane, axis=1), picked)
            here = here | found
        gap = obs[0] - picked
        total = total + jnp.where(here, obs[2] * gap * gap, 0.0)
    at_slot = lax.broadcasted_iota(jnp.int32, (TILE, LANES), 1) == par * slots + slot
    misfit[...] = jnp.where(at_slot, jnp.sum(total), 0.0)


def forecast(own, got, direct, passed, near, far, obs_own, obs_got, piece, slot, slots, ncol, total_rows):
    parts = plan(ncol, slot, slots)
    _, worked, kept = parts[piece]
    place = []
    for ct in worked:
        p = 0 if ct in parts[0][0] else 1
        place.append((p, parts[p][0].index(ct)))
    block = jax.ShapeDtypeStruct((3, TILE, len(kept) * LANES), jnp.float32)
    field = pltpu.VMEM((3, len(worked), ROWS, LANES), jnp.float32)
    args = [own, direct, *got, *passed, near, far, obs_own, obs_got]
    return pl.pallas_call(
        functools.partial(
            forecast_kernel,
            worked=worked,
            kept=kept,
            place=place,
            parts=len(got),
            slot=slot,
            slots=slots,
            ncol=ncol,
            total_rows=total_rows,
        ),
        out_shape=[block, block, jax.ShapeDtypeStruct((TILE, LANES), jnp.float32)],
        in_specs=[VMEM] * len(args),
        out_specs=[VMEM] * 3,
        scratch_shapes=[field, field, field, pltpu.VMEM((ROWS, LANES), jnp.float32)],
        compiler_params=pltpu.CompilerParams(vmem_limit_bytes=24 * 2**20),
        cost_estimate=cost(WORK * len(worked)),
    )(*args)


def gather_kernel(*refs, ncol, slots, pieces):
    out = refs[-1]
    par = lax.axis_index("strip") % 2
    for n, (k, p) in enumerate(pieces):
        mine, theirs = refs[2 * n], refs[2 * n + 1]
        for j, ct in enumerate(plan(ncol, k, slots)[p][2]):
            out[par * slots + k, :, :, at(ct)] = mine[:, :, at(j)]
            out[(1 - par) * slots + k, :, :, at(ct)] = theirs[:, :, at(j)]


def gather(blocks, pieces, ncol, slots):
    args = [b for pair in blocks for b in pair]
    return pl.pallas_call(
        functools.partial(gather_kernel, ncol=ncol, slots=slots, pieces=pieces),
        out_shape=jax.ShapeDtypeStruct((2 * slots, 3, TILE, ncol * LANES), jnp.float32),
        in_specs=[VMEM] * len(args),
        out_specs=VMEM,
        compiler_params=pltpu.CompilerParams(vmem_limit_bytes=SMALL),
        cost_estimate=cost(0.1),
    )(*args)


def local(ensemble, offspring, observations, obs_cols, obs_precision):
    members, _, strip_rows, cols = ensemble.shape
    strips = lax.axis_size("strip")
    total_rows = strips * strip_rows
    strip = lax.axis_index("strip")
    half = members // 2
    ncol = cols // LANES

    def moved(even, odd):
        return [(i, (i + (odd if i % 2 else even)) % strips) for i in range(strips)]

    swap = moved(1, -1)
    straight = moved(-2, 2)
    onward = moved(2, -2)
    cross = moved(3, -3)

    arrived = lax.ppermute(ensemble, "particle", [(0, 1), (1, 0)])
    index = sources(offspring, ensemble)

    rows = (strip * strip_rows + jnp.arange(strip_rows, dtype=jnp.int32)).astype(jnp.float32)
    weight = obs_precision * (1.0 + 2.0 * (rows + 0.5) / total_rows)[:, None]
    obs_own = jnp.stack([observations, obs_cols.astype(jnp.float32), weight])

    spans = [
        [(sent[0] * LANES, len(sent) * LANES) for sent, _, _ in plan(ncol, k, half)]
        for k in range(half)
    ]
    kept, given, near, far = pick(index, ensemble, arrived, spans)
    near = lax.ppermute(near, "strip", onward)
    far = lax.ppermute(far, "strip", cross)

    obs_got = lax.ppermute(obs_own, "strip", swap)

    pieces = [(k, p) for k in range(half) for p in range(len(spans[k]))]
    got, passed, direct, blocks, misfits = [], [], [], [], []
    first = None
    for k in range(half):
        giving, keeping = tuple(given[k]), kept[k]
        if k:
            giving = after(giving, first)
        got.append([lax.ppermute(g, "strip", swap) for g in giving])
        if k:
            (keeping,) = after((keeping,), (got[k], obs_got))
        direct.append(lax.ppermute(keeping, "strip", straight))
        passed.append([lax.ppermute(g, "strip", onward) for g in got[k]])
        if first is None:
            first = (got[0], near, far)
    for k, p in pieces:
        (own,) = after((kept[k],), (got[-1], misfits[-1:]))
        keep, send, misfit = forecast(
            own,
            got[k][: p + 1],
            direct[k],
            passed[k][: p + 1],
            near,
            far,
            obs_own,
            obs_got,
            p,
            k,
            half,
            ncol,
            total_rows,
        )
        blocks.append((keep, lax.ppermute(send, "strip", swap)))
        misfits.append(misfit)
    total = sum(misfits[1:], misfits[0])
    (total,) = after((total,), [b[1] for b in blocks[:-1]])
    if strips == 8:
        turn = [lax.ppermute(total, "strip", moved(step, step)) for step in (2, 4, 6)]
        total = (total + turn[1]) + (turn[0] + turn[2])
    else:
        step = 2
        while step < strips:
            total = total + lax.ppermute(total, "strip", [(i, i ^ step) for i in range(strips)])
            step *= 2
    theirs = lax.ppermute(total, "strip", swap)
    state = gather(blocks, pieces, ncol, half)
    theirs, total = after((theirs, total), state)
    total = total + theirs
    log_weights = (-0.5 / (total_rows * obs_cols.shape[1])) * total[0, :members]
    return (state, log_weights)


def solution(mesh):
    in_specs = (
        P(("group", "particle"), None, "strip", None),
        P("group"),
        P(("group", "strip"), None),
        P(("group", "strip"), None),
        P(("group", "strip"), None),
    )
    out_specs = (P(("group", "particle"), None, "strip", None), P(("group", "particle")))
    return jax.shard_map(local, mesh=mesh, in_specs=in_specs, out_specs=out_specs, check_vma=False)
```

```python
import functools

import jax
import jax.numpy as jnp
from jax import lax
from jax.experimental import pallas as pl
from jax.experimental.pallas import tpu as pltpu
from jax.sharding import PartitionSpec as P

STEPS = 3
DT = 0.4
HALF = 0.5 * DT
DEPTH = 3 * STEPS
LANES = 128
TILE = 8
BASE = 16
ROWS = 48
SMALL = 12 * 2**20
WORK = 0.005

VMEM = pl.BlockSpec(memory_space=pltpu.VMEM)
SMEM = pl.BlockSpec(memory_space=pltpu.SMEM)
ANY = pl.BlockSpec(memory_space=pl.ANY)


def cost(us):
    return pl.CostEstimate(flops=0, bytes_accessed=int(us * 3.0e6), transcendentals=0)


def plan(ncol, slot, slots):
    every = list(range(ncol))
    if slot < slots - 1:
        return ((every, every, every),)
    cut = ncol // 2 + 2
    return (
        (every[:cut], every[:cut], every[1 : cut - 1]),
        (every[cut:], every[cut - 2 :] + [0, 1], every[cut - 1 :] + [0]),
    )


def after(arrays, first):
    return lax.optimization_barrier((tuple(arrays), first))[0]


def at(i):
    return slice(i * LANES, (i + 1) * LANES)


def index_kernel(offspring, ensemble, index):
    members = index.shape[0]
    here = lax.axis_index("particle")
    cumulative = []
    for i in range(offspring.shape[0]):
        cumulative.append(offspring[i] + (cumulative[-1] if i else 0))
    for k in range(members):
        j = here * members + k
        s = sum((c <= j).astype(jnp.int32) for c in cumulative)
        own = s - here * members
        other = s - (1 - here) * members
        inside = (own >= 0) & (own < members)
        index[k] = jnp.clip(jnp.where(inside, own, members + other), 0, 2 * members - 1)


def sources(offspring, ensemble):
    members = ensemble.shape[0]
    return pl.pallas_call(
        index_kernel,
        out_shape=jax.ShapeDtypeStruct((members,), jnp.int32),
        in_specs=[SMEM, VMEM],
        out_specs=SMEM,
        compiler_params=pltpu.CompilerParams(vmem_limit_bytes=SMALL),
    )(offspring, ensemble)


def pick_kernel(index, own, other, *outs, spans):
    members = own.shape[0]
    half = members // 2
    par = lax.axis_index("strip") % 2
    refs, kept, given = list(outs), [], []
    for s in spans:
        kept.append([refs.pop(0)])
        given.append([refs.pop(0) for _ in s])
    near, far = refs
    wide = own.shape[3] // TILE

    def copy(slot, k, pieces, edge):
        i = index[slot]

        def write(ref, m):
            if len(pieces) == 1:
                pieces[0][...] = ref[m]
            else:
                for (first, count), out in zip(spans[k], pieces):
                    out[...] = ref[m, :, :, pl.ds(first, count)]

            def edges(row):
                for f in range(3):
                    for q in range(TILE):
                        edge[k * 3 + f, q : q + 1, :] = ref[
                            m, f, row : row + 1, q * wide : (q + 1) * wide
                        ]

            @pl.when(par == 0)
            def _():
                edges(TILE - 1)

            @pl.when(par == 1)
            def _():
                edges(0)

        @pl.when(i < members)
        def _():
            write(own, jnp.minimum(i, members - 1))

        @pl.when(i >= members)
        def _():
            write(other, jnp.maximum(i - members, 0))

    for k in range(half):
        copy((1 - par) * half + k, k, given[k], far)
        copy(par * half + k, k, kept[k], near)


def pick(index, own, other, spans):
    shape, kind = own.shape[1:3], own.dtype
    outs = []
    for s in spans:
        outs += [jax.ShapeDtypeStruct(shape + (c,), kind) for c in [own.shape[3]] + [c for _, c in s]]
    outs += [jax.ShapeDtypeStruct((3 * len(spans), TILE, own.shape[3] // TILE), kind)] * 2
    out = pl.pallas_call(
        functools.partial(pick_kernel, spans=spans),
        out_shape=outs,
        in_specs=[SMEM, VMEM, VMEM],
        out_specs=[VMEM] * len(outs),
        compiler_params=pltpu.CompilerParams(vmem_limit_bytes=SMALL),
    )(index, own, other)
    kept, given = [], []
    for s in spans:
        kept.append(out[0])
        given.append(out[1 : 1 + len(s)])
        out = out[1 + len(s) :]
    return kept, given, out[0], out[1]


def evaluate(src, state, dst, cor_ref, start, tiles, kind):
    ncol = src.shape[1]
    lane = lax.broadcasted_iota(jnp.int32, (TILE, LANES), 1)
    first = lane == 0
    last = lane == LANES - 1

    def body(t, carry):
        r0 = start + t * TILE
        rows = pl.ds(r0, TILE)
        cor = cor_ref[rows, :]
        for ct in range(ncol):
            mid, around = [], []
            for f in range(3):
                c = src[f, ct, rows, :]
                e = pltpu.roll(
                    jnp.where(first, src[f, (ct + 1) % ncol, rows, :], c), LANES - 1, 1
                )
                w = pltpu.roll(jnp.where(last, src[f, (ct - 1) % ncol, rows, :], c), 1, 1)
                n = src[f, ct, pl.ds(r0 + 1, TILE), :]
                s = src[f, ct, pl.ds(r0 - 1, TILE), :]
                mid.append(c)
                around.append((e, w, n, s))
            eta, u, v = mid
            (eE, eW, eN, eS), (uE, uW, uN, uS), (vE, vW, vN, vS) = around
            duy = uN - uS
            dvx = vE - vW
            dux = uE - uW
            dvy = vN - vS
            flow = (dux + dvy) + ((eE * uE - eW * uW) + (eN * vN - eS * vS))
            lu = v * (cor - duy) - u * dux - (eE - eW)
            lv = u * (cor + dvx) + v * dvy + (eN - eS)
            change = (-flow, lu, -lv)
            for f in range(3):
                if kind == 0:
                    new = mid[f] + HALF * change[f]
                elif kind == 1:
                    new = 0.75 * state[f, ct, rows, :] + (0.25 * mid[f] + (0.25 * HALF) * change[f])
                else:
                    new = (1.0 / 3.0) * state[f, ct, rows, :] + (
                        (2.0 / 3.0) * mid[f] + (2.0 / 3.0 * HALF) * change[f]
                    )
                dst[f, ct, rows, :] = new
        return carry

    lax.fori_loop(0, tiles, body, 0)


def forecast_kernel(*refs, worked, kept, place, parts, slot, slots, ncol, total_rows):
    own, direct, refs = refs[0], refs[1], refs[2:]
    got, passed = refs[:parts], refs[parts : 2 * parts]
    near, far, obs_own, obs_got, keep, send, misfit, state, s1, s2, cor_ref = refs[2 * parts :]
    strip = lax.axis_index("strip")
    par = strip % 2
    per = ncol // TILE

    def load(own_row, got_row, direct_row, passed_row, near_row, far_row):
        for i, ct in enumerate(worked):
            p, j = place[i]
            for ref, row, place_at in (
                (own, own_row, ct),
                (got[p], got_row, j),
                (direct, direct_row, ct),
                (passed[p], passed_row, j),
            ):
                state[:, i, row : row + TILE, :] = ref[:, :, at(place_at)]
            for ref, row in ((near, near_row), (far, far_row)):
                q = ct // per
                state[:, i, row : row + 1, :] = ref[
                    slot * 3 : slot * 3 + 3, q : q + 1, at(ct % per)
                ]

    above, below = BASE - TILE, BASE + 2 * TILE

    @pl.when(par == 0)
    def _():
        load(BASE, BASE + TILE, below, above, above - 1, below + TILE)

    @pl.when(par == 1)
    def _():
        load(BASE + TILE, BASE, above, below, below + TILE, above - 1)

    row = lax.broadcasted_iota(jnp.int32, (ROWS, LANES), 0) + ((strip - par) * TILE - BASE)
    row = jnp.where(row < 0, row + total_rows, row)
    row = jnp.where(row >= total_rows, row - total_rows, row).astype(jnp.float32)
    cor_ref[...] = 2.0 * (0.3 + 0.4 * ((row + 0.5) / total_rows - 0.5))

    for k in range(DEPTH):
        reach = DEPTH - 1 - k
        tiles = (2 * TILE + 2 * reach + TILE - 1) // TILE
        kind = k % 3
        src, dst = ((state, s1), (s1, s2), (s2, state))[kind]
        evaluate(src, state, dst, cor_ref, BASE - reach, tiles, kind)

    def store(keep_row, send_row):
        for j, ct in enumerate(kept):
            i = worked.index(ct)
            keep[:, :, at(j)] = state[:, i, keep_row : keep_row + TILE, :]
            send[:, :, at(j)] = state[:, i, send_row : send_row + TILE, :]

    @pl.when(par == 0)
    def _():
        store(BASE, BASE + TILE)

    @pl.when(par == 1)
    def _():
        store(BASE + TILE, BASE)

    total = jnp.zeros((TILE, LANES), jnp.float32)
    for side in range(2):
        mine = par == side
        obs = [jnp.where(mine, obs_own[k], obs_got[k]) for k in range(3)]
        where = obs[1].astype(jnp.int32)
        tile, lane = where // LANES, where % LANES
        picked = jnp.zeros((TILE, LANES), jnp.float32)
        here = jnp.zeros((TILE, LANES), jnp.bool_)
        for ct in kept:
            i = worked.index(ct)
            eta = state[0, i, BASE + side * TILE : BASE + (side + 1) * TILE, :]
            found = tile == ct
            picked = jnp.where(found, jnp.take_along_axis(eta, lane, axis=1), picked)
            here = here | found
        gap = obs[0] - picked
        total = total + jnp.where(here, obs[2] * gap * gap, 0.0)
    at_slot = lax.broadcasted_iota(jnp.int32, (TILE, LANES), 1) == par * slots + slot
    misfit[...] = jnp.where(at_slot, jnp.sum(total), 0.0)


def forecast(own, got, direct, passed, near, far, obs_own, obs_got, piece, slot, slots, ncol, total_rows):
    parts = plan(ncol, slot, slots)
    _, worked, kept = parts[piece]
    place = []
    for ct in worked:
        p = 0 if ct in parts[0][0] else 1
        place.append((p, parts[p][0].index(ct)))
    block = jax.ShapeDtypeStruct((3, TILE, len(kept) * LANES), jnp.float32)
    field = pltpu.VMEM((3, len(worked), ROWS, LANES), jnp.float32)
    args = [own, direct, *got, *passed, near, far, obs_own, obs_got]
    return pl.pallas_call(
        functools.partial(
            forecast_kernel,
            worked=worked,
            kept=kept,
            place=place,
            parts=len(got),
            slot=slot,
            slots=slots,
            ncol=ncol,
            total_rows=total_rows,
        ),
        out_shape=[block, block, jax.ShapeDtypeStruct((TILE, LANES), jnp.float32)],
        in_specs=[VMEM] * len(args),
        out_specs=[VMEM] * 3,
        scratch_shapes=[field, field, field, pltpu.VMEM((ROWS, LANES), jnp.float32)],
        compiler_params=pltpu.CompilerParams(vmem_limit_bytes=24 * 2**20),
        cost_estimate=cost(WORK * len(worked)),
    )(*args)


def gather_kernel(*refs, ncol, slots, pieces):
    out = refs[-1]
    par = lax.axis_index("strip") % 2
    for n, (k, p) in enumerate(pieces):
        mine, theirs = refs[2 * n], refs[2 * n + 1]
        for j, ct in enumerate(plan(ncol, k, slots)[p][2]):
            out[par * slots + k, :, :, at(ct)] = mine[:, :, at(j)]
            out[(1 - par) * slots + k, :, :, at(ct)] = theirs[:, :, at(j)]


def gather(blocks, pieces, ncol, slots):
    args = [b for pair in blocks for b in pair]
    return pl.pallas_call(
        functools.partial(gather_kernel, ncol=ncol, slots=slots, pieces=pieces),
        out_shape=jax.ShapeDtypeStruct((2 * slots, 3, TILE, ncol * LANES), jnp.float32),
        in_specs=[VMEM] * len(args),
        out_specs=VMEM,
        compiler_params=pltpu.CompilerParams(vmem_limit_bytes=SMALL),
        cost_estimate=cost(0.1),
    )(*args)


def local(ensemble, offspring, observations, obs_cols, obs_precision):
    members, _, strip_rows, cols = ensemble.shape
    strips = lax.axis_size("strip")
    total_rows = strips * strip_rows
    strip = lax.axis_index("strip")
    half = members // 2
    ncol = cols // LANES

    def moved(even, odd):
        return [(i, (i + (odd if i % 2 else even)) % strips) for i in range(strips)]

    swap = moved(1, -1)
    straight = moved(-2, 2)
    onward = moved(2, -2)
    cross = moved(3, -3)

    arrived = lax.ppermute(ensemble, "particle", [(0, 1), (1, 0)])
    index = sources(offspring, ensemble)

    rows = (strip * strip_rows + jnp.arange(strip_rows, dtype=jnp.int32)).astype(jnp.float32)
    weight = obs_precision * (1.0 + 2.0 * (rows + 0.5) / total_rows)[:, None]
    obs_own = jnp.stack([observations, obs_cols.astype(jnp.float32), weight])

    spans = [
        [(sent[0] * LANES, len(sent) * LANES) for sent, _, _ in plan(ncol, k, half)]
        for k in range(half)
    ]
    kept, given, near, far = pick(index, ensemble, arrived, spans)
    near = lax.ppermute(near, "strip", onward)
    far = lax.ppermute(far, "strip", cross)

    obs_got = lax.ppermute(obs_own, "strip", swap)

    pieces = [(k, p) for k in range(half) for p in range(len(spans[k]))]
    got, passed, direct, blocks, misfits = [], [], [], [], []
    first = None
    for k in range(half):
        giving, keeping = tuple(given[k]), kept[k]
        if k:
            giving = after(giving, first)
        got.append([lax.ppermute(g, "strip", swap) for g in giving])
        if k:
            (keeping,) = after((keeping,), (got[k], obs_got))
        direct.append(lax.ppermute(keeping, "strip", straight))
        passed.append([lax.ppermute(g, "strip", onward) for g in got[k]])
        if first is None:
            first = (got[0], near, far)
    for k, p in pieces:
        (own,) = after((kept[k],), (got[-1], misfits[-1:]))
        keep, send, misfit = forecast(
            own,
            got[k][: p + 1],
            direct[k],
            passed[k][: p + 1],
            near,
            far,
            obs_own,
            obs_got,
            p,
            k,
            half,
            ncol,
            total_rows,
        )
        blocks.append((keep, lax.ppermute(send, "strip", swap)))
        misfits.append(misfit)
    total = sum(misfits[1:], misfits[0])
    (total,) = after((total,), [b[1] for b in blocks[:-1]])
    state = gather(blocks, pieces, ncol, half)
    if strips == 8:
        turn = [lax.ppermute(total, "strip", moved(step, step)) for step in (2, 4, 6)]
        *turn, total = after((*turn, total), state)
        total = (total + turn[1]) + (turn[0] + turn[2])
    else:
        step = 2
        while step < strips:
            total = total + lax.ppermute(total, "strip", [(i, i ^ step) for i in range(strips)])
            step *= 2
    total = total + lax.ppermute(total, "strip", swap)
    log_weights = (-0.5 / (total_rows * obs_cols.shape[1])) * total[0, :members]
    return (state, log_weights)


def solution(mesh):
    in_specs = (
        P(("group", "particle"), None, "strip", None),
        P("group"),
        P(("group", "strip"), None),
        P(("group", "strip"), None),
        P(("group", "strip"), None),
    )
    out_specs = (P(("group", "particle"), None, "strip", None), P(("group", "particle")))
    return jax.shard_map(local, mesh=mesh, in_specs=in_specs, out_specs=out_specs, check_vma=False)
```

```python
import functools

import jax
import jax.numpy as jnp
from jax import lax
from jax.experimental import pallas as pl
from jax.experimental.pallas import tpu as pltpu
from jax.sharding import PartitionSpec as P

STEPS = 3
DT = 0.4
HALF = 0.5 * DT
DEPTH = 3 * STEPS
LANES = 128
TILE = 8
BASE = 16
ROWS = 48
SMALL = 12 * 2**20
WORK = 0.005

VMEM = pl.BlockSpec(memory_space=pltpu.VMEM)
SMEM = pl.BlockSpec(memory_space=pltpu.SMEM)
ANY = pl.BlockSpec(memory_space=pl.ANY)


def cost(us):
    return pl.CostEstimate(flops=0, bytes_accessed=int(us * 3.0e6), transcendentals=0)


def plan(ncol, slot, slots):
    every = list(range(ncol))
    if slot < slots - 1:
        return ((every, every, every),)
    cut = ncol * 11 // 16
    return (
        (every[:cut], every[:cut], every[1 : cut - 1]),
        (every[cut:], every[cut - 2 :] + [0, 1], every[cut - 1 :] + [0]),
    )


def after(arrays, first):
    return lax.optimization_barrier((tuple(arrays), first))[0]


def at(i):
    return slice(i * LANES, (i + 1) * LANES)


def index_kernel(offspring, ensemble, index):
    members = index.shape[0]
    here = lax.axis_index("particle")
    cumulative = []
    for i in range(offspring.shape[0]):
        cumulative.append(offspring[i] + (cumulative[-1] if i else 0))
    for k in range(members):
        j = here * members + k
        s = sum((c <= j).astype(jnp.int32) for c in cumulative)
        own = s - here * members
        other = s - (1 - here) * members
        inside = (own >= 0) & (own < members)
        index[k] = jnp.clip(jnp.where(inside, own, members + other), 0, 2 * members - 1)


def sources(offspring, ensemble):
    members = ensemble.shape[0]
    return pl.pallas_call(
        index_kernel,
        out_shape=jax.ShapeDtypeStruct((members,), jnp.int32),
        in_specs=[SMEM, VMEM],
        out_specs=SMEM,
        compiler_params=pltpu.CompilerParams(vmem_limit_bytes=SMALL),
    )(offspring, ensemble)


def pick_kernel(index, own, other, *outs, spans):
    members = own.shape[0]
    half = members // 2
    par = lax.axis_index("strip") % 2
    refs, kept, given = list(outs), [], []
    for s in spans:
        kept.append([refs.pop(0)])
        given.append([refs.pop(0) for _ in s])
    near, far = refs
    wide = own.shape[3] // TILE

    def copy(slot, k, pieces, edge):
        i = index[slot]

        def write(ref, m):
            if len(pieces) == 1:
                pieces[0][...] = ref[m]
            else:
                for (first, count), out in zip(spans[k], pieces):
                    out[...] = ref[m, :, :, pl.ds(first, count)]

            def edges(row):
                for f in range(3):
                    for q in range(TILE):
                        edge[k * 3 + f, q : q + 1, :] = ref[
                            m, f, row : row + 1, q * wide : (q + 1) * wide
                        ]

            @pl.when(par == 0)
            def _():
                edges(TILE - 1)

            @pl.when(par == 1)
            def _():
                edges(0)

        @pl.when(i < members)
        def _():
            write(own, jnp.minimum(i, members - 1))

        @pl.when(i >= members)
        def _():
            write(other, jnp.maximum(i - members, 0))

    for k in range(half):
        copy((1 - par) * half + k, k, given[k], far)
        copy(par * half + k, k, kept[k], near)


def pick(index, own, other, spans):
    shape, kind = own.shape[1:3], own.dtype
    outs = []
    for s in spans:
        outs += [jax.ShapeDtypeStruct(shape + (c,), kind) for c in [own.shape[3]] + [c for _, c in s]]
    outs += [jax.ShapeDtypeStruct((3 * len(spans), TILE, own.shape[3] // TILE), kind)] * 2
    out = pl.pallas_call(
        functools.partial(pick_kernel, spans=spans),
        out_shape=outs,
        in_specs=[SMEM, VMEM, VMEM],
        out_specs=[VMEM] * len(outs),
        compiler_params=pltpu.CompilerParams(vmem_limit_bytes=SMALL),
    )(index, own, other)
    kept, given = [], []
    for s in spans:
        kept.append(out[0])
        given.append(out[1 : 1 + len(s)])
        out = out[1 + len(s) :]
    return kept, given, out[0], out[1]


def evaluate(src, state, dst, cor_ref, start, tiles, kind):
    ncol = src.shape[1]
    lane = lax.broadcasted_iota(jnp.int32, (TILE, LANES), 1)
    first = lane == 0
    last = lane == LANES - 1

    def body(t, carry):
        r0 = start + t * TILE
        rows = pl.ds(r0, TILE)
        cor = cor_ref[rows, :]
        for ct in range(ncol):
            mid, around = [], []
            for f in range(3):
                c = src[f, ct, rows, :]
                e = pltpu.roll(
                    jnp.where(first, src[f, (ct + 1) % ncol, rows, :], c), LANES - 1, 1
                )
                w = pltpu.roll(jnp.where(last, src[f, (ct - 1) % ncol, rows, :], c), 1, 1)
                n = src[f, ct, pl.ds(r0 + 1, TILE), :]
                s = src[f, ct, pl.ds(r0 - 1, TILE), :]
                mid.append(c)
                around.append((e, w, n, s))
            eta, u, v = mid
            (eE, eW, eN, eS), (uE, uW, uN, uS), (vE, vW, vN, vS) = around
            duy = uN - uS
            dvx = vE - vW
            dux = uE - uW
            dvy = vN - vS
            flow = (dux + dvy) + ((eE * uE - eW * uW) + (eN * vN - eS * vS))
            lu = v * (cor - duy) - u * dux - (eE - eW)
            lv = u * (cor + dvx) + v * dvy + (eN - eS)
            change = (-flow, lu, -lv)
            for f in range(3):
                if kind == 0:
                    new = mid[f] + HALF * change[f]
                elif kind == 1:
                    new = 0.75 * state[f, ct, rows, :] + (0.25 * mid[f] + (0.25 * HALF) * change[f])
                else:
                    new = (1.0 / 3.0) * state[f, ct, rows, :] + (
                        (2.0 / 3.0) * mid[f] + (2.0 / 3.0 * HALF) * change[f]
                    )
                dst[f, ct, rows, :] = new
        return carry

    lax.fori_loop(0, tiles, body, 0)


def forecast_kernel(*refs, worked, kept, place, parts, slot, slots, ncol, total_rows):
    own, direct, refs = refs[0], refs[1], refs[2:]
    got, passed = refs[:parts], refs[parts : 2 * parts]
    near, far, obs_own, obs_got, keep, send, misfit, state, s1, s2, cor_ref = refs[2 * parts :]
    strip = lax.axis_index("strip")
    par = strip % 2
    per = ncol // TILE

    def load(own_row, got_row, direct_row, passed_row, near_row, far_row):
        for i, ct in enumerate(worked):
            p, j = place[i]
            for ref, row, place_at in (
                (own, own_row, ct),
                (got[p], got_row, j),
                (direct, direct_row, ct),
                (passed[p], passed_row, j),
            ):
                state[:, i, row : row + TILE, :] = ref[:, :, at(place_at)]
            for ref, row in ((near, near_row), (far, far_row)):
                q = ct // per
                state[:, i, row : row + 1, :] = ref[
                    slot * 3 : slot * 3 + 3, q : q + 1, at(ct % per)
                ]

    above, below = BASE - TILE, BASE + 2 * TILE

    @pl.when(par == 0)
    def _():
        load(BASE, BASE + TILE, below, above, above - 1, below + TILE)

    @pl.when(par == 1)
    def _():
        load(BASE + TILE, BASE, above, below, below + TILE, above - 1)

    row = lax.broadcasted_iota(jnp.int32, (ROWS, LANES), 0) + ((strip - par) * TILE - BASE)
    row = jnp.where(row < 0, row + total_rows, row)
    row = jnp.where(row >= total_rows, row - total_rows, row).astype(jnp.float32)
    cor_ref[...] = 2.0 * (0.3 + 0.4 * ((row + 0.5) / total_rows - 0.5))

    for k in range(DEPTH):
        reach = DEPTH - 1 - k
        tiles = (2 * TILE + 2 * reach + TILE - 1) // TILE
        kind = k % 3
        src, dst = ((state, s1), (s1, s2), (s2, state))[kind]
        evaluate(src, state, dst, cor_ref, BASE - reach, tiles, kind)

    def store(keep_row, send_row):
        for j, ct in enumerate(kept):
            i = worked.index(ct)
            keep[:, :, at(j)] = state[:, i, keep_row : keep_row + TILE, :]
            send[:, :, at(j)] = state[:, i, send_row : send_row + TILE, :]

    @pl.when(par == 0)
    def _():
        store(BASE, BASE + TILE)

    @pl.when(par == 1)
    def _():
        store(BASE + TILE, BASE)

    total = jnp.zeros((TILE, LANES), jnp.float32)
    for side in range(2):
        mine = par == side
        obs = [jnp.where(mine, obs_own[k], obs_got[k]) for k in range(3)]
        where = obs[1].astype(jnp.int32)
        tile, lane = where // LANES, where % LANES
        picked = jnp.zeros((TILE, LANES), jnp.float32)
        here = jnp.zeros((TILE, LANES), jnp.bool_)
        for ct in kept:
            i = worked.index(ct)
            eta = state[0, i, BASE + side * TILE : BASE + (side + 1) * TILE, :]
            found = tile == ct
            picked = jnp.where(found, jnp.take_along_axis(eta, lane, axis=1), picked)
            here = here | found
        gap = obs[0] - picked
        total = total + jnp.where(here, obs[2] * gap * gap, 0.0)
    at_slot = lax.broadcasted_iota(jnp.int32, (TILE, LANES), 1) == par * slots + slot
    misfit[...] = jnp.where(at_slot, jnp.sum(total), 0.0)


def forecast(own, got, direct, passed, near, far, obs_own, obs_got, piece, slot, slots, ncol, total_rows):
    parts = plan(ncol, slot, slots)
    _, worked, kept = parts[piece]
    place = []
    for ct in worked:
        p = 0 if ct in parts[0][0] else 1
        place.append((p, parts[p][0].index(ct)))
    block = jax.ShapeDtypeStruct((3, TILE, len(kept) * LANES), jnp.float32)
    field = pltpu.VMEM((3, len(worked), ROWS, LANES), jnp.float32)
    args = [own, direct, *got, *passed, near, far, obs_own, obs_got]
    return pl.pallas_call(
        functools.partial(
            forecast_kernel,
            worked=worked,
            kept=kept,
            place=place,
            parts=len(got),
            slot=slot,
            slots=slots,
            ncol=ncol,
            total_rows=total_rows,
        ),
        out_shape=[block, block, jax.ShapeDtypeStruct((TILE, LANES), jnp.float32)],
        in_specs=[VMEM] * len(args),
        out_specs=[VMEM] * 3,
        scratch_shapes=[field, field, field, pltpu.VMEM((ROWS, LANES), jnp.float32)],
        compiler_params=pltpu.CompilerParams(vmem_limit_bytes=24 * 2**20),
        cost_estimate=cost(WORK * len(worked)),
    )(*args)


def gather_kernel(*refs, ncol, slots, pieces):
    out = refs[-1]
    par = lax.axis_index("strip") % 2
    for n, (k, p) in enumerate(pieces):
        mine, theirs = refs[2 * n], refs[2 * n + 1]
        for j, ct in enumerate(plan(ncol, k, slots)[p][2]):
            out[par * slots + k, :, :, at(ct)] = mine[:, :, at(j)]
            out[(1 - par) * slots + k, :, :, at(ct)] = theirs[:, :, at(j)]


def gather(blocks, pieces, ncol, slots):
    args = [b for pair in blocks for b in pair]
    return pl.pallas_call(
        functools.partial(gather_kernel, ncol=ncol, slots=slots, pieces=pieces),
        out_shape=jax.ShapeDtypeStruct((2 * slots, 3, TILE, ncol * LANES), jnp.float32),
        in_specs=[VMEM] * len(args),
        out_specs=VMEM,
        compiler_params=pltpu.CompilerParams(vmem_limit_bytes=SMALL),
        cost_estimate=cost(0.1),
    )(*args)


def local(ensemble, offspring, observations, obs_cols, obs_precision):
    members, _, strip_rows, cols = ensemble.shape
    strips = lax.axis_size("strip")
    total_rows = strips * strip_rows
    strip = lax.axis_index("strip")
    half = members // 2
    ncol = cols // LANES

    def moved(even, odd):
        return [(i, (i + (odd if i % 2 else even)) % strips) for i in range(strips)]

    swap = moved(1, -1)
    straight = moved(-2, 2)
    onward = moved(2, -2)
    cross = moved(3, -3)

    arrived = lax.ppermute(ensemble, "particle", [(0, 1), (1, 0)])
    index = sources(offspring, ensemble)

    rows = (strip * strip_rows + jnp.arange(strip_rows, dtype=jnp.int32)).astype(jnp.float32)
    weight = obs_precision * (1.0 + 2.0 * (rows + 0.5) / total_rows)[:, None]
    obs_own = jnp.stack([observations, obs_cols.astype(jnp.float32), weight])

    spans = [
        [(sent[0] * LANES, len(sent) * LANES) for sent, _, _ in plan(ncol, k, half)]
        for k in range(half)
    ]
    kept, given, near, far = pick(index, ensemble, arrived, spans)
    near = lax.ppermute(near, "strip", onward)
    far = lax.ppermute(far, "strip", cross)

    obs_got = lax.ppermute(obs_own, "strip", swap)

    pieces = [(k, p) for k in range(half) for p in range(len(spans[k]))]
    got, passed, direct, blocks, misfits = [], [], [], [], []
    first = None
    for k in range(half):
        giving, keeping = tuple(given[k]), kept[k]
        if k:
            giving = after(giving, first)
        got.append([lax.ppermute(g, "strip", swap) for g in giving])
        if k:
            (keeping,) = after((keeping,), (got[k], obs_got))
        direct.append(lax.ppermute(keeping, "strip", straight))
        passed.append([lax.ppermute(g, "strip", onward) for g in got[k]])
        if first is None:
            first = (got[0], near, far)
    for k, p in pieces:
        (own,) = after((kept[k],), (got[-1], misfits[-1:]))
        keep, send, misfit = forecast(
            own,
            got[k][: p + 1],
            direct[k],
            passed[k][: p + 1],
            near,
            far,
            obs_own,
            obs_got,
            p,
            k,
            half,
            ncol,
            total_rows,
        )
        blocks.append((keep, lax.ppermute(send, "strip", swap)))
        misfits.append(misfit)
    total = sum(misfits[1:], misfits[0])
    (total,) = after((total,), [b[1] for b in blocks[:-1]])
    state = gather(blocks, pieces, ncol, half)
    if strips == 8:
        turn = [lax.ppermute(total, "strip", moved(step, step)) for step in (2, 4, 6)]
        *turn, total = after((*turn, total), state)
        total = (total + turn[1]) + (turn[0] + turn[2])
    else:
        step = 2
        while step < strips:
            total = total + lax.ppermute(total, "strip", [(i, i ^ step) for i in range(strips)])
            step *= 2
    total = total + lax.ppermute(total, "strip", swap)
    log_weights = (-0.5 / (total_rows * obs_cols.shape[1])) * total[0, :members]
    return (state, log_weights)


def solution(mesh):
    in_specs = (
        P(("group", "particle"), None, "strip", None),
        P("group"),
        P(("group", "strip"), None),
        P(("group", "strip"), None),
        P(("group", "strip"), None),
    )
    out_specs = (P(("group", "particle"), None, "strip", None), P(("group", "particle")))
    return jax.shard_map(local, mesh=mesh, in_specs=in_specs, out_specs=out_specs, check_vma=False)
```
